32 devices in a mesh: ta: 4 (over y, x), sa: 8 (over z, core).
Axes of the slice: x: 2, y: 2, z: 4, core: 2. Of those that a mesh axis runs over, the one named last changes fastest.
Arguments:
- snapshots: float32 [256, 2, 32768], P('ta', None, 'sa'), may hold values from -6 to 6
- bins: int32 [16], replicated, may hold values from 0 to 127, as said below
- eigenvalues: float32 [16, 32], P('ta'), may hold values from 100 to 1000
- old_basis: bfloat16 [16, 2, 32, 2, 32768], P('ta', None, None, None, 'sa'), may hold values from -0.015625 to 0.015625, as said below
- block_count: int32 [1], replicated, may hold values from 1 to 8
Outputs:
- new_basis: bfloat16 [16, 2, 32, 2, 32768], P('ta', None, None, None, 'sa')
- coherence: float32 [16, 2, 32, 32], P('ta')
The draws below stay inside these ranges and needn't reach their ends.
Inputs may be any that keep to these rules, and one draw needn't show every extreme that they name: The 16 bins are distinct; 0 and 127 are always among them. `old_basis`: every entry lies within 4 / sqrt(65536) in magnitude.
All inputs are finite; a program needn't handle non-finite values.
Results may differ from the reference program's by a relative error of at most 0.001.
Values sent between devices are 32-bit elements; how exact they have to be, the bound alone decides.
A program may use at most 128 MiB of HBM per device.

```python
import math
import jax
import jax.numpy as jnp
from jax import lax

NT = 256
NBINS = 16
RANK = 32
NS = 32768


def draw_bins(key, part):
    half = NT // 2
    inner = jax.random.permutation(key, half - 2)[:NBINS - 2].astype(jnp.int32) + 1
    full = jnp.concatenate([jnp.array([0, half - 1], jnp.int32), inner])
    order = jax.random.permutation(jax.random.fold_in(key, 7), NBINS)
    return full[order]


def draw_old_basis(key, part):
    own_key = jax.random.fold_in(key, 11)
    common_key = jax.random.fold_in(key, 12)
    angle_key = jax.random.fold_in(key, 13)
    shape = (NBINS, 2, RANK, 2, NS)
    common_shape = (NBINS, 2, 2, NS)
    own = jnp.clip(jax.random.normal(own_key, shape, jnp.float32), -4.0, 4.0)
    common = jnp.clip(jax.random.normal(common_key, common_shape, jnp.float32), -4.0, 4.0)
    share = 0.5
    theta = jax.random.uniform(angle_key, (NBINS, RANK), jnp.float32, -math.pi, math.pi)
    cosine = jnp.cos(theta)[:, :, None, None]
    sine = jnp.sin(theta)[:, :, None, None]
    common_re = common[:, 0][:, None, :, :]
    common_im = common[:, 1][:, None, :, :]
    rotated_re = common_re * cosine - common_im * sine
    rotated_im = common_re * sine + common_im * cosine
    rotated = jnp.stack([rotated_re, rotated_im], axis=1)
    limit = 4.0 * (1.0 - 2.0 ** (-8))
    mixed = jnp.clip(own + share * rotated, -limit, limit)
    return (mixed * (2.0 * NS) ** (-0.5)).astype(jnp.bfloat16)


def block_levels(key, shape, cuts, smallest, high):
    loudness = 1.0
    for axis_at, parts in cuts:
        steps = jax.random.uniform(jax.random.fold_in(jax.random.fold_in(key, 6), axis_at), (parts,), jnp.float32, smallest / len(cuts), high / len(cuts))
        loudness = loudness * jnp.repeat(jnp.exp(steps), shape[axis_at] // parts).reshape((-1,) + (1,) * (len(shape) - 1 - axis_at))
    return loudness


def gaussian(key, dims, scale, most, split=(), kind=jnp.bfloat16):
    level = block_levels(key, dims, split, -0.22, 0.18) if split else 1.0
    values = jax.random.normal(key, dims, jnp.float32) * scale * level
    return jnp.minimum(jnp.maximum(values, -most), most).astype(kind)


def setup_inputs(seed: int = 0) -> dict:
    splits = jax.random.split(jax.random.key(seed), 6)
    snapshots = gaussian(splits[0], (NT, 2, NS), 1.0, 6.0, ((0, 4), (2, 8)), jnp.float32)
    bins = draw_bins(jax.random.fold_in(splits[5], 71), 0)
    eigenvalues = jnp.clip(jnp.exp(math.log(1000.0) - 2.3025851 * jax.random.uniform(splits[2], (NBINS, RANK), jnp.float32) ** block_levels(splits[2], (NBINS, RANK), ((0, 4),), -0.2, 0.2)), 100.0, 1000.0)
    old_basis = draw_old_basis(jax.random.fold_in(splits[5], 71), 0)
    block_count = jax.random.randint(splits[4], (1,), 1, 9).astype(jnp.int32)
    return {"snapshots": snapshots, "bins": bins, "eigenvalues": eigenvalues, "old_basis": old_basis, "block_count": block_count}


def tables(bins, times, total):
    phase = bins[:, None] * times[None, :] % total
    angle = 2.0 * math.pi / total * phase.astype(jnp.float32)
    window = 0.5 - 0.5 * jnp.cos(2.0 * math.pi / total * times.astype(jnp.float32))
    scale = math.sqrt(8.0 / (3.0 * total))
    return (jnp.cos(angle) * window[None, :] * scale, -jnp.sin(angle) * window[None, :] * scale)

def update_bin(basis, spec, lam, w_old, w_new):
    hi = lax.Precision.HIGHEST
    u_re = basis[0].astype(jnp.float32)
    u_im = basis[1].astype(jnp.float32)
    s_re = spec[0]
    s_im = spec[1]
    c_re = jnp.dot(u_re, s_re, precision=hi) + jnp.dot(u_im, s_im, precision=hi)
    c_im = jnp.dot(u_re, s_im, precision=hi) - jnp.dot(u_im, s_re, precision=hi)
    scaled = w_old * lam
    g_re = scaled[:, None] * u_re + w_new * (c_re[:, None] * s_re[None, :] + c_im[:, None] * s_im[None, :])
    g_im = scaled[:, None] * u_im + w_new * (c_re[:, None] * s_im[None, :] - c_im[:, None] * s_re[None, :])
    gram_re = jnp.dot(g_re, g_re.T, precision=hi) + jnp.dot(g_im, g_im.T, precision=hi)
    gram_im = jnp.dot(g_re, g_im.T, precision=hi) - jnp.dot(g_im, g_re.T, precision=hi)
    inv = 1.0 / jnp.sqrt(jnp.diagonal(gram_re) + 1e-06)
    fresh = jnp.stack([g_re * inv[:, None], g_im * inv[:, None]]).astype(jnp.bfloat16)
    outer = inv[:, None] * inv[None, :]
    return (fresh, jnp.stack([gram_re * outer, gram_im * outer]))

def reference(snapshots, bins, eigenvalues, old_basis, block_count):
    total = snapshots.shape[0]
    points = snapshots.shape[2]
    times = jnp.arange(total, dtype=jnp.int32)
    c_tab, s_tab = tables(bins, times, total)
    flat = snapshots.reshape(total, 2 * points)
    hi = lax.Precision.HIGHEST
    spec = jnp.stack([jnp.dot(c_tab, flat, precision=hi), jnp.dot(s_tab, flat, precision=hi)], axis=1)
    count = block_count[0].astype(jnp.float32)
    w_old = count / (count + 1.0)
    w_new = 1.0 / (count + 1.0)
    basis = old_basis.reshape(old_basis.shape[0], 2, old_basis.shape[2], 2 * points)

    def one(items):
        return update_bin(items[0], items[1], items[2], w_old, w_new)
    fresh, coherence = lax.map(one, (basis, spec, eigenvalues))
    return (fresh.reshape(old_basis.shape), coherence)
```

```python
import functools
import math

import jax
import jax.numpy as jnp
from jax import lax
from jax.experimental import pallas as pl
from jax.experimental.pallas import tpu as pltpu
from jax.sharding import PartitionSpec as P

MESH = pl.DeviceIdType.MESH
BF = jnp.bfloat16
F32 = jnp.float32
CHUNKS = 8


def exact(a, b):
    return jnp.dot(a, b, precision=lax.Precision.HIGHEST, preferred_element_type=F32)


def exact_nt(a, b):
    return lax.dot_general(
        a, b, (((1,), (1,)), ((), ())), precision=lax.Precision.HIGHEST, preferred_element_type=F32
    )


def dot_nt(a, b):
    return lax.dot_general(a, b, (((1,), (1,)), ((), ())), preferred_element_type=F32)


def split(x):
    high = x.astype(BF)
    return high, (x - high.astype(F32)).astype(BF)


def iota(shape, axis):
    return lax.broadcasted_iota(jnp.int32, shape, axis)


def exchange(groups, spread, bins_ref, snap_ref, basis_ref, spec_ref, coef_ref, gram_ref,
             xs, ub, terms, recv, cbuf, gbuf, in_sem, rs_send, rs_recv, g_send, g_recv, c_send, c_recv):
    slice_len = snap_ref.shape[0]
    points = snap_ref.shape[2]
    nb, _, rank = basis_ref.shape[:3]
    nbins = bins_ref.shape[0]
    rows = 4 * rank
    step = points // CHUNKS
    total = slice_len * groups
    me_t = lax.axis_index("ta")
    me_s = lax.axis_index("sa")
    loads = [
        pltpu.make_async_copy(
            snap_ref.at[:, v, pl.ds(h * (points // 2), points // 2)],
            xs.at[v, :, pl.ds(h * (points // 2), points // 2)], in_sem.at[2 * h + v])
        for h in range(2) for v in range(2)
    ]
    for load in loads:
        load.start()
    load_basis = pltpu.make_async_copy(
        basis_ref.reshape(nb * rows, points), ub, in_sem.at[4])
    load_basis.start()

    barrier = pltpu.get_barrier_semaphore()
    for d in range(1, groups):
        pl.semaphore_signal(barrier, inc=1, device_id=(lax.rem(me_t + d, groups), me_s), device_id_type=MESH)
    for d in range(1, spread):
        pl.semaphore_signal(barrier, inc=1, device_id=(me_t, lax.rem(me_s + d, spread)), device_id_type=MESH)

    row = iota((2 * nbins, slice_len), 0)
    t = iota((2 * nbins, slice_len), 1) + me_t * slice_len
    bin_of = jnp.zeros((2 * nbins, slice_len), jnp.int32)
    for b in range(nbins):
        bin_of = jnp.where(row // 2 == b, bins_ref[b], bin_of)
    phase = jnp.bitwise_and(bin_of * t + (row % 2) * (total // 4), total - 1)
    unit = 2.0 * math.pi / total
    window = 0.5 - 0.5 * jnp.cos(unit * t.astype(F32))
    table = jnp.cos(unit * phase.astype(F32)) * window * math.sqrt(8.0 / (3.0 * total))
    th, tl = split(table)
    left = jnp.concatenate(
        [jnp.concatenate([th, th], axis=1), jnp.concatenate([tl, jnp.zeros_like(tl)], axis=1)], axis=0)

    pl.semaphore_wait(barrier, groups - 1 + spread - 1)

    sends = []
    for k in range(CHUNKS):
        if k == 0:
            loads[0].wait()
            loads[1].wait()
        if k == CHUNKS // 2:
            loads[2].wait()
            loads[3].wait()
        cols = pl.ds(k * step, step)
        for v in range(2):
            xh, xl = split(xs[v, :, cols])
            out = jnp.dot(left, jnp.concatenate([xh, xl], axis=0), preferred_element_type=F32)
            out = out[: 2 * nbins] + out[2 * nbins:]
            terms[:, v, :, cols] = out.reshape(groups, 2 * nb, step)
        for d in range(1, groups):
            peer = lax.rem(me_t + d, groups)
            copy = pltpu.make_async_remote_copy(
                src_ref=terms.at[peer, :, :, cols], dst_ref=recv.at[d - 1, :, :, cols],
                send_sem=rs_send.at[k, d - 1], recv_sem=rs_recv.at[k, d - 1],
                device_id=(peer, me_s), device_id_type=MESH)
            copy.start()
            sends.append(copy)

    load_basis.wait()
    ri, ci = iota((rows, rows), 0), iota((rows, rows), 1)
    same_v = (ri % 2) == (ci % 2)
    same_c = (ri // (2 * rank)) == (ci // (2 * rank))
    one = jnp.ones((rows, rows), F32)
    keep_re = jnp.where(jnp.logical_and(same_v, same_c), one, 0.0)
    keep_im = jnp.where(jnp.logical_and(same_v, jnp.logical_not(same_c)),
                        jnp.where(ri < 2 * rank, one, -one), 0.0)
    mode = (ri // 2) % rank
    fold = jnp.where(iota((rank, rows), 0) == (iota((rank, rows), 1) // 2) % rank, 1.0, 0.0)
    for p in range(nb // 2):
        wide = jnp.zeros((rows, rows), F32)
        for h in range(2):
            w = ub[pl.ds((2 * p + h) * rows, rows), :]
            m = dot_nt(w, w)
            wide += exact(m * keep_re, jnp.where(ci == mode + 2 * h * rank, 1.0, 0.0))
            wide += exact(m * keep_im, jnp.where(ci == mode + (2 * h + 1) * rank, 1.0, 0.0))
        gbuf[me_s, p] = exact(fold, wide)
    g_copies = []
    for d in range(1, spread):
        copy = pltpu.make_async_remote_copy(
            src_ref=gbuf.at[me_s], dst_ref=gbuf.at[me_s], send_sem=g_send.at[d], recv_sem=g_recv.at[d],
            device_id=(me_t, lax.rem(me_s + d, spread)), device_id_type=MESH)
        copy.start()
        g_copies.append(copy)

    acc = jnp.zeros((8 * nb, nb * rows), F32)
    square = jnp.zeros((2 * nb, 128), F32)
    for k in range(CHUNKS):
        cols = pl.ds(k * step, step)
        for d in range(1, groups):
            sends[k * (groups - 1) + d - 1].wait_recv()
        spec = terms[me_t, :, :, cols]
        for d in range(1, groups):
            spec = spec + recv[d - 1, :, :, cols]
        spec_ref[:, :, cols] = spec
        sq = spec[0] * spec[0] + spec[1] * spec[1]
        for i in range(step // 128):
            square = square + sq[:, i * 128:(i + 1) * 128]
        flat = spec.reshape(4 * nb, step)
        sh, sl = split(flat)
        acc = acc + dot_nt(jnp.concatenate([sh, sl], axis=0), ub[:, cols])
    ar, ac = iota(acc.shape, 0), iota(acc.shape, 1)
    match = jnp.logical_and((ar // 2) % nb == ac // rows, (ar // (2 * nb)) % 2 == ac % 2)
    c_col = (ac // (2 * rank)) % 2
    same = ar % 2 == c_col
    a_re = jnp.where(jnp.logical_and(match, same), acc, 0.0)
    a_im = jnp.where(jnp.logical_and(match, jnp.logical_not(same)), jnp.where(c_col == 0, acc, -acc), 0.0)
    qr, qc = iota((2 * nb, 8 * nb), 0), iota((2 * nb, 8 * nb), 1)
    q_bin = qr // 2 == (qc // 2) % nb
    q_re = jnp.where(jnp.logical_and(q_bin, qr % 2 == 0), 1.0, 0.0)
    q_im = jnp.where(jnp.logical_and(q_bin, qr % 2 == 1), 1.0, 0.0)
    er, ec = iota((nb * rows, 128), 0), iota((nb * rows, 128), 1)
    pick = jnp.where((er // 2) % rank == ec, 1.0, 0.0)
    coef = exact(exact(q_re, a_re) + exact(q_im, a_im), pick)
    norm = jnp.sum(square, axis=1, keepdims=True)
    cbuf[me_s] = jnp.where(iota((2 * nb, 128), 1) == rank, norm, coef)
    c_copies = []
    for d in range(1, spread):
        copy = pltpu.make_async_remote_copy(
            src_ref=cbuf.at[me_s], dst_ref=cbuf.at[me_s], send_sem=c_send.at[d], recv_sem=c_recv.at[d],
            device_id=(me_t, lax.rem(me_s + d, spread)), device_id_type=MESH)
        copy.start()
        c_copies.append(copy)
    for copy in g_copies:
        copy.wait_recv()
    gram = gbuf[0]
    for s in range(1, spread):
        gram = gram + gbuf[s]
    gram_ref[...] = gram
    for copy in c_copies:
        copy.wait_recv()
    coef = cbuf[0]
    for s in range(1, spread):
        coef = coef + cbuf[s]
    coef_ref[...] = coef
    for copy in sends + g_copies + c_copies:
        copy.wait_send()


def update(count_ref, eig_ref, coef_ref, gram_ref, spec_ref, basis_ref, fresh_ref, coh_ref, ub, ob, in_sem, out_sem):
    nb, _, rank = basis_ref.shape[:3]
    points = basis_ref.shape[4]
    rows = 4 * rank
    flat_in = basis_ref.reshape(nb * rows, points)
    flat_out = fresh_ref.reshape(nb * rows, points)
    loads = [pltpu.make_async_copy(flat_in.at[pl.ds(b * rows, rows), :], ub.at[pl.ds(b * rows, rows), :], in_sem.at[b])
             for b in range(nb)]
    stores = [pltpu.make_async_copy(ob.at[pl.ds(b * rows, rows), :], flat_out.at[pl.ds(b * rows, rows), :], out_sem.at[b])
              for b in range(nb)]
    for load in loads:
        load.start()
    count = jnp.full((1, 1), count_ref[0], jnp.int32).astype(F32)
    w_old = count / (count + 1.0)
    w_new = 1.0 / (count + 1.0)
    scaled = w_old * eig_ref[...]
    coef = coef_ref[...]
    coef_t = jnp.transpose(coef)
    scaled_t = jnp.transpose(jnp.concatenate([scaled, scaled], axis=0))
    eye = iota((rank, rank), 0) == iota((rank, rank), 1)
    r8 = iota((2 * nb, rank), 0)
    k_p = jnp.zeros((2 * nb, rank), F32)
    k_s = jnp.zeros((2 * nb, rank), F32)
    k_a = jnp.zeros((2 * nb, rank), F32)
    for b in range(nb):
        g = gram_ref[b // 2]
        at = 2 * rank * (b % 2)
        g_re, g_im = g[:, at:at + rank], g[:, at + rank:at + 2 * rank]
        cr, ci = coef[2 * b:2 * b + 1, :rank], coef[2 * b + 1:2 * b + 2, :rank]
        cr_c, ci_c = coef_t[:rank, 2 * b:2 * b + 1], coef_t[:rank, 2 * b + 1:2 * b + 2]
        norm = coef[2 * b:2 * b + 1, rank:rank + 1] + coef[2 * b + 1:2 * b + 2, rank:rank + 1]
        a, a_c = scaled[b:b + 1], scaled_t[:, b:b + 1]
        weight = w_new * (a_c + a) + (w_new * w_new) * norm
        pair = a_c * a
        full_re = pair * g_re + weight * (cr_c * cr + ci_c * ci)
        full_im = pair * g_im + weight * (ci_c * cr - cr_c * ci)
        diag = jnp.where(eye, full_re, 0.0)
        inv = 1.0 / jnp.sqrt(jnp.sum(diag, axis=0, keepdims=True) + 1e-06)
        inv_c = 1.0 / jnp.sqrt(jnp.sum(diag, axis=1, keepdims=True) + 1e-06)
        outer = inv_c * inv
        coh_ref[b, 0] = full_re * outer
        coh_ref[b, 1] = full_im * outer
        p_row, q_row = inv * w_new * cr, inv * w_new * ci
        k_p = jnp.where(r8 == 2 * b, p_row, jnp.where(r8 == 2 * b + 1, q_row, k_p))
        k_s = jnp.where(r8 == 2 * b, -q_row, jnp.where(r8 == 2 * b + 1, p_row, k_s))
        k_a = jnp.where(r8 == 2 * b, inv * a, k_a)
    wide = 12 * nb
    er, ec = iota((nb * rows, rank), 0), iota((nb * rows, rank), 1)
    pick = jnp.where((er // 2) % rank == ec, 1.0, 0.0)
    t_p = exact_nt(pick, jnp.concatenate([k_p] * 6, axis=0))
    t_s = exact_nt(pick, jnp.concatenate([k_s] * 6, axis=0))
    t_a = exact_nt(pick, k_a)
    rr, rc = iota((nb * rows, wide), 0), iota((nb * rows, wide), 1)
    match = jnp.logical_and(rr // rows == (rc // 2) % nb, rr % 2 == (rc // (2 * nb)) % 2)
    mix = jnp.where(match, jnp.where((rr // (2 * rank)) % 2 == 0, t_p, t_s), 0.0)
    mh = mix.astype(BF)
    left = jnp.where(rc < 8 * nb, mh.astype(F32), mix - mh.astype(F32)).astype(BF)
    r2, c2 = iota((nb * rows, 2 * nb), 0), iota((nb * rows, 2 * nb), 1)
    gain = jnp.sum(jnp.where(r2 // rows == c2 // 2, t_a, 0.0), axis=1, keepdims=True)
    sh, sl = split(spec_ref[...].reshape(4 * nb, points))
    right = jnp.concatenate([sh, sl, sh], axis=0)
    step = 512
    for b in range(nb):
        loads[b].wait()
        at = pl.ds(b * rows, rows)
        lb, gb = left[b * rows:(b + 1) * rows], gain[b * rows:(b + 1) * rows]
        for k in range(points // step):
            cols = pl.ds(k * step, step)
            add = jnp.dot(lb, right[:, k * step:(k + 1) * step], preferred_element_type=F32)
            ob[at, cols] = (gb * ub[at, cols].astype(F32) + add).astype(BF)
        stores[b].start()
    for store in stores:
        store.wait()


def local(groups, spread, snapshots, bins, eigenvalues, old_basis, block_count):
    slice_len, _, points = snapshots.shape
    nb, _, rank = old_basis.shape[:3]
    rows = 4 * rank
    vmem = pl.BlockSpec(memory_space=pltpu.VMEM)
    smem = pl.BlockSpec(memory_space=pltpu.SMEM)
    hbm = pl.BlockSpec(memory_space=pl.ANY)
    spec, coef, gram = pl.pallas_call(
        functools.partial(exchange, groups, spread),
        out_shape=(
            jax.ShapeDtypeStruct((2, 2 * nb, points), F32),
            jax.ShapeDtypeStruct((2 * nb, 128), F32),
            jax.ShapeDtypeStruct((nb // 2, rank, 128), F32),
        ),
        in_specs=[smem, hbm, hbm],
        out_specs=(vmem, vmem, vmem),
        scratch_shapes=[
            pltpu.VMEM((2, slice_len, points), F32),
            pltpu.VMEM((nb * rows, points), BF),
            pltpu.VMEM((groups, 2, 2 * nb, points), F32),
            pltpu.VMEM((groups - 1, 2, 2 * nb, points), F32),
            pltpu.VMEM((spread, 2 * nb, 128), F32),
            pltpu.VMEM((spread, nb // 2, rank, 128), F32),
            pltpu.SemaphoreType.DMA((5,)),
            pltpu.SemaphoreType.DMA((CHUNKS, groups - 1)),
            pltpu.SemaphoreType.DMA((CHUNKS, groups - 1)),
            pltpu.SemaphoreType.DMA((spread,)),
            pltpu.SemaphoreType.DMA((spread,)),
            pltpu.SemaphoreType.DMA((spread,)),
            pltpu.SemaphoreType.DMA((spread,)),
        ],
        compiler_params=pltpu.CompilerParams(
            collective_id=0, has_side_effects=True, vmem_limit_bytes=40 * 2**20),
        name="exchange",
    )(bins, snapshots, old_basis)
    fresh, coherence = pl.pallas_call(
        update,
        out_shape=(
            jax.ShapeDtypeStruct(old_basis.shape, BF),
            jax.ShapeDtypeStruct((nb, 2, rank, rank), F32),
        ),
        in_specs=[smem, vmem, vmem, vmem, vmem, hbm],
        out_specs=(hbm, vmem),
        scratch_shapes=[
            pltpu.VMEM((nb * rows, points), BF),
            pltpu.VMEM((nb * rows, points), BF),
            pltpu.SemaphoreType.DMA((nb,)),
            pltpu.SemaphoreType.DMA((nb,)),
        ],
        compiler_params=pltpu.CompilerParams(vmem_limit_bytes=40 * 2**20),
        name="update",
    )(block_count, eigenvalues, coef, gram, spec, old_basis)
    return fresh, coherence


def solution(mesh):
    groups, spread = mesh.shape["ta"], mesh.shape["sa"]
    return jax.shard_map(
        functools.partial(local, groups, spread),
        mesh=mesh,
        in_specs=(P("ta", None, "sa"), P(), P("ta", None), P("ta", None, None, None, "sa"), P()),
        out_specs=(P("ta", None, None, None, "sa"), P("ta", None, None, None)),
        check_vma=False,
    )
```

```python
import functools
import math

import jax
import jax.numpy as jnp
from jax import lax
from jax.experimental import pallas as pl
from jax.experimental.pallas import tpu as pltpu
from jax.sharding import PartitionSpec as P

MESH = pl.DeviceIdType.MESH
BF = jnp.bfloat16
F32 = jnp.float32
CHUNKS = 8
LIMIT = 40 * 2**20


def dot_nt(a, b):
    return lax.dot_general(a, b, (((1,), (1,)), ((), ())), preferred_element_type=F32)


def split(x):
    high = x.astype(BF)
    return high, (x - high.astype(F32)).astype(BF)


def split3(x):
    high = x.astype(BF)
    rest = x - high.astype(F32)
    mid = rest.astype(BF)
    return high, mid, (rest - mid.astype(F32)).astype(BF)


def right_pick(x, pick):
    n = x.shape[0]
    out = jnp.dot(jnp.concatenate(split3(x), axis=0), pick, preferred_element_type=F32)
    return out[:n] + out[n:2 * n] + out[2 * n:]


def iota(shape, axis):
    return lax.broadcasted_iota(jnp.int32, shape, axis)


def ones_where(mask):
    return jnp.where(mask, 1.0, 0.0).astype(BF)


def exchange(groups, spread, bins_ref, snap_ref, basis_ref, spec_ref, coef_ref, gram_ref,
             bins, xs, ub, terms, recv, fwd, cbuf, gbuf, in_sem, rs_send, rs_recv, g_send, g_recv, c_send, c_recv):
    assert groups == 4
    slice_len = snap_ref.shape[0]
    points = snap_ref.shape[2]
    nb, _, rank = basis_ref.shape[:3]
    nbins = bins_ref.shape[0]
    rows = 4 * rank
    step = points // CHUNKS
    total = slice_len * groups
    me_t = lax.axis_index("ta")
    me_s = lax.axis_index("sa")
    load_bins = pltpu.make_async_copy(bins_ref, bins, in_sem.at[5])
    load_bins.start()
    loads = [
        pltpu.make_async_copy(
            snap_ref.at[:, v, pl.ds(h * (points // 2), points // 2)],
            xs.at[v, :, pl.ds(h * (points // 2), points // 2)], in_sem.at[2 * h + v])
        for h in range(2) for v in range(2)
    ]
    for load in loads:
        load.start()
    load_basis = pltpu.make_async_copy(
        basis_ref.reshape(nb * rows, points), ub, in_sem.at[4])
    load_basis.start()

    near = me_t + 1 - 2 * lax.rem(me_t, 2)
    far = lax.rem(me_t + 2, 4)
    diagonal = lax.rem(near + 2, 4)
    barrier = pltpu.get_barrier_semaphore()
    for peer in (near, far):
        pl.semaphore_signal(barrier, inc=1, device_id=(peer, me_s), device_id_type=MESH)
    for d in range(1, spread):
        pl.semaphore_signal(barrier, inc=1, device_id=(me_t, lax.rem(me_s + d, spread)), device_id_type=MESH)

    t = iota((2 * nbins, slice_len), 1) + me_t * slice_len
    row = iota((2 * nbins, slice_len), 0)
    unit = 2.0 * math.pi / total
    window = (0.5 - 0.5 * jnp.cos(unit * t[:8].astype(F32))) * math.sqrt(8.0 / (3.0 * total))
    window = jnp.concatenate([window] * (2 * nbins // 8), axis=0)
    load_bins.wait()
    bin_of = jnp.zeros((2 * nbins, slice_len), jnp.int32)
    for b in range(nbins):
        bin_of = jnp.where(row // 2 == b, bins[b], bin_of)
    phase = jnp.bitwise_and(bin_of * t + (row % 2) * (total // 4), total - 1)
    th, tl = split(jnp.cos(unit * phase.astype(F32)) * window)
    left = jnp.concatenate(
        [jnp.concatenate([th, th], axis=1), jnp.concatenate([tl, jnp.zeros_like(tl)], axis=1)], axis=0)

    pl.semaphore_wait(barrier, 2 + spread - 1)

    def rs_copy(src, slot, v, k, peer):
        cols = pl.ds(k * step, step)
        return pltpu.make_async_remote_copy(
            src_ref=src.at[v, :, cols], dst_ref=recv.at[slot, v, :, cols],
            send_sem=rs_send.at[k, v, slot], recv_sem=rs_recv.at[k, v, slot],
            device_id=(peer, me_s), device_id_type=MESH)

    first, second = (near, far), (far, near)
    copies = {}
    for k in range(CHUNKS):
        if k == 0:
            loads[0].wait()
            loads[1].wait()
        if k == CHUNKS // 2:
            loads[2].wait()
            loads[3].wait()
        cols = pl.ds(k * step, step)
        for v in range(2):
            xh, xl = split(xs[v, :, cols])
            out = jnp.dot(left, jnp.concatenate([xh, xl], axis=0), preferred_element_type=F32)
            out = out[: 2 * nbins] + out[2 * nbins:]
            terms[:, v, :, cols] = out.reshape(groups, 2 * nb, step)
            copies[k, v, 0] = rs_copy(terms.at[diagonal], 0, v, k, first[v])
            copies[k, v, 1] = rs_copy(terms.at[first[v]], 1, v, k, first[v])
            copies[k, v, 0].start()
            copies[k, v, 1].start()

    def pass_on(k):
        cols = pl.ds(k * step, step)
        for v in range(2):
            copies[k, v, 0].wait_recv()
            fwd[v, :, cols] = terms[second[v], v, :, cols] + recv[0, v, :, cols]
            copies[k, v, 2] = rs_copy(fwd, 2, v, k, second[v])
            copies[k, v, 2].start()

    load_basis.wait()
    two = 2 * rows
    ri, ci = iota((two, two), 0), iota((two, two), 1)
    same_v = jnp.logical_and((ri % 2) == (ci % 2), ri // rows == ci // rows)
    r_c, c_c = (ri // (2 * rank)) % 2, (ci // (2 * rank)) % 2
    keep_re = jnp.where(jnp.logical_and(same_v, r_c == c_c), 1.0, 0.0)
    keep_im = jnp.where(jnp.logical_and(same_v, r_c != c_c), jnp.where(r_c == 0, 1.0, -1.0), 0.0)
    pr, pc = iota((2 * two, 128), 0), iota((2 * two, 128), 1)
    place = ones_where(pc == (pr // 2) % rank + 2 * rank * ((pr // rows) % 2) + rank * (pr // two))
    fold = ones_where(iota((rank, 3 * two), 0) == (iota((rank, 3 * two), 1) // 2) % rank)
    for p in range(nb // 2):
        w = ub[pl.ds(p * two, two), :]
        big = dot_nt(w, w)
        for k in range(p * CHUNKS // nb, (p + 1) * CHUNKS // nb):
            pass_on(k)
        wide = right_pick(jnp.concatenate([big * keep_re, big * keep_im], axis=1), place)
        gbuf[me_s, p] = jnp.dot(fold, jnp.concatenate(split3(wide), axis=0), preferred_element_type=F32)
    g_copies = []
    for d in range(1, spread):
        copy = pltpu.make_async_remote_copy(
            src_ref=gbuf.at[me_s], dst_ref=gbuf.at[me_s], send_sem=g_send.at[d], recv_sem=g_recv.at[d],
            device_id=(me_t, lax.rem(me_s + d, spread)), device_id_type=MESH)
        copy.start()
        g_copies.append(copy)
    for k in range((nb // 2) * CHUNKS // nb, CHUNKS):
        pass_on(k)

    er, ec = iota((nb * rows, 128), 0), iota((nb * rows, 128), 1)
    pick = ones_where((er // 2) % rank == ec)
    acc = jnp.zeros((8 * nb, nb * rows), F32)
    square = jnp.zeros((2 * nb, 128), F32)
    for k in range(CHUNKS):
        cols = pl.ds(k * step, step)
        for v in range(2):
            copies[k, v, 1].wait_recv()
            copies[k, v, 2].wait_recv()
        spec = terms[me_t, :, :, cols] + recv[1, :, :, cols] + recv[2, :, :, cols]
        sq = spec[0] * spec[0] + spec[1] * spec[1]
        for i in range(step // 128):
            square = square + sq[:, i * 128:(i + 1) * 128]
        both = jnp.concatenate(split(spec.reshape(4 * nb, step)), axis=0)
        spec_ref[:, cols] = both
        acc = acc + dot_nt(both, ub[:, cols])
    acc = acc[: 4 * nb] + acc[4 * nb:]
    ar, ac = iota((2 * nb, nb * rows), 0), iota((2 * nb, nb * rows), 1)
    acc = jnp.where(ac % 2 == 0, acc[: 2 * nb], acc[2 * nb:])
    even = ar % 2 == 0
    other = jnp.where(even, pltpu.roll(acc, 2 * nb - 1, 0), -pltpu.roll(acc, 1, 0))
    acc = jnp.where((ac // (2 * rank)) % 2 == 0, acc, other)
    coef = right_pick(jnp.where(ar // 2 == ac // rows, acc, 0.0), pick)
    norm = jnp.sum(square, axis=1, keepdims=True)
    cbuf[me_s] = jnp.where(iota((2 * nb, 128), 1) == rank, norm, coef)
    c_copies = []
    for d in range(1, spread):
        copy = pltpu.make_async_remote_copy(
            src_ref=cbuf.at[me_s], dst_ref=cbuf.at[me_s], send_sem=c_send.at[d], recv_sem=c_recv.at[d],
            device_id=(me_t, lax.rem(me_s + d, spread)), device_id_type=MESH)
        copy.start()
        c_copies.append(copy)
    for copy in g_copies:
        copy.wait_recv()
    gram = gbuf[0]
    for s in range(1, spread):
        gram = gram + gbuf[s]
    gram_ref[...] = gram
    for copy in list(copies.values()) + g_copies:
        copy.wait_send()
    for copy in c_copies:
        copy.wait_recv()
    coef = cbuf[0]
    for s in range(1, spread):
        coef = coef + cbuf[s]
    coef_ref[...] = coef
    for copy in c_copies:
        copy.wait_send()


def update(count_ref, eig_ref, coef_ref, gram_ref, spec_ref, basis_ref, fresh_ref, coh_ref, ub, ob, in_sem, out_sem):
    nb, _, rank = basis_ref.shape[:3]
    points = basis_ref.shape[4]
    rows = 4 * rank
    flat_in = basis_ref.reshape(nb * rows, points)
    flat_out = fresh_ref.reshape(nb * rows, points)
    step = points // CHUNKS
    parts = [pl.ds(k * step, step) for k in range(CHUNKS)]
    loads = [pltpu.make_async_copy(flat_in.at[:, p], ub.at[:, p], in_sem.at[k]) for k, p in enumerate(parts)]
    stores = [pltpu.make_async_copy(ob.at[:, p], flat_out.at[:, p], out_sem.at[k]) for k, p in enumerate(parts)]
    for load in loads:
        load.start()
    count = jnp.full((1, 1), count_ref[0], jnp.int32).astype(F32)
    w_old = count / (count + 1.0)
    w_new = 1.0 / (count + 1.0)
    scaled = w_old * eig_ref[...]
    coef = coef_ref[...]
    coef_t = jnp.transpose(coef)
    scaled_t = jnp.transpose(jnp.concatenate([scaled, scaled], axis=0))
    eye = iota((rank, rank), 0) == iota((rank, rank), 1)
    r8 = iota((2 * nb, 128), 0)
    k_p = jnp.zeros((2 * nb, 128), F32)
    k_s = jnp.zeros((2 * nb, 128), F32)
    k_a = jnp.zeros((2 * nb, 128), F32)
    pad = jnp.zeros((1, 128 - rank), F32)
    for b in range(nb):
        g = gram_ref[b // 2]
        at = 2 * rank * (b % 2)
        g_re, g_im = g[:, at:at + rank], g[:, at + rank:at + 2 * rank]
        cr, ci = coef[2 * b:2 * b + 1, :rank], coef[2 * b + 1:2 * b + 2, :rank]
        cr_c, ci_c = coef_t[:rank, 2 * b:2 * b + 1], coef_t[:rank, 2 * b + 1:2 * b + 2]
        norm = coef[2 * b:2 * b + 1, rank:rank + 1] + coef[2 * b + 1:2 * b + 2, rank:rank + 1]
        a, a_c = scaled[b:b + 1], scaled_t[:, b:b + 1]
        weight = w_new * (a_c + a) + (w_new * w_new) * norm
        pair = a_c * a
        full_re = pair * g_re + weight * (cr_c * cr + ci_c * ci)
        full_im = pair * g_im + weight * (ci_c * cr - cr_c * ci)
        diag = jnp.where(eye, full_re, 0.0)
        inv = 1.0 / jnp.sqrt(jnp.sum(diag, axis=0, keepdims=True) + 1e-06)
        inv_c = 1.0 / jnp.sqrt(jnp.sum(diag, axis=1, keepdims=True) + 1e-06)
        outer = inv_c * inv
        coh_ref[b, 0] = full_re * outer
        coh_ref[b, 1] = full_im * outer
        p_row = jnp.concatenate([inv * w_new * cr, pad], axis=1)
        q_row = jnp.concatenate([inv * w_new * ci, pad], axis=1)
        a_row = jnp.concatenate([inv * a, pad], axis=1)
        k_p = jnp.where(r8 == 2 * b, p_row, jnp.where(r8 == 2 * b + 1, q_row, k_p))
        k_s = jnp.where(r8 == 2 * b, -q_row, jnp.where(r8 == 2 * b + 1, p_row, k_s))
        k_a = jnp.where(r8 == 2 * b, a_row, k_a)
    wide = 12 * nb
    lane = iota((2 * nb, 128), 1)
    k_mix = jnp.where(lane < rank, k_p, pltpu.roll(k_s, rank, 1))
    k_gain = jnp.where(lane < rank, k_a, pltpu.roll(k_a, rank, 1))
    er, ec = iota((nb * rows, 128), 0), iota((nb * rows, 128), 1)
    pick = ones_where((er // 2) % (2 * rank) == ec)
    values = jnp.concatenate([k_mix] * 6 + [k_gain], axis=0)
    spread_out = dot_nt(jnp.concatenate([pick] * 3, axis=1), jnp.concatenate(split3(values), axis=1))
    rr, rc = iota(spread_out.shape, 0), iota(spread_out.shape, 1)
    match = rr // rows == (rc // 2) % nb
    gain = jnp.sum(jnp.where(jnp.logical_and(match, jnp.logical_and(rc >= wide, rc % 2 == 0)), spread_out, 0.0),
                   axis=1, keepdims=True)
    match = jnp.logical_and(match, rr % 2 == (rc // (2 * nb)) % 2)
    mix = jnp.where(match, spread_out, 0.0)[:, :wide]
    mh = mix.astype(BF).astype(F32)
    left = jnp.where(rc[:, :wide] < 8 * nb, mh, mix - mh).astype(BF)
    for k, cols in enumerate(parts):
        right = jnp.concatenate([spec_ref[:, cols], spec_ref[: 4 * nb, cols]], axis=0)
        add = jnp.dot(left, right, preferred_element_type=F32)
        loads[k].wait()
        ob[:, cols] = (gain * ub[:, cols].astype(F32) + add).astype(BF)
        stores[k].start()
    for store in stores:
        store.wait()


def local(groups, spread, snapshots, bins, eigenvalues, old_basis, block_count):
    slice_len, _, points = snapshots.shape
    nb, _, rank = old_basis.shape[:3]
    rows = 4 * rank
    vmem = pl.BlockSpec(memory_space=pltpu.VMEM)
    smem = pl.BlockSpec(memory_space=pltpu.SMEM)
    hbm = pl.BlockSpec(memory_space=pl.ANY)
    spec, coef, gram = pl.pallas_call(
        functools.partial(exchange, groups, spread),
        out_shape=(
            jax.ShapeDtypeStruct((8 * nb, points), BF),
            jax.ShapeDtypeStruct((2 * nb, 128), F32),
            jax.ShapeDtypeStruct((nb // 2, rank, 128), F32),
        ),
        in_specs=[pl.BlockSpec(memory_space=pltpu.HBM)] * 3,
        out_specs=(vmem, vmem, vmem),
        scratch_shapes=[
            pltpu.SMEM(bins.shape, jnp.int32),
            pltpu.VMEM((2, slice_len, points), F32),
            pltpu.VMEM((nb * rows, points), BF),
            pltpu.VMEM((groups, 2, 2 * nb, points), F32),
            pltpu.VMEM((3, 2, 2 * nb, points), F32),
            pltpu.VMEM((2, 2 * nb, points), F32),
            pltpu.VMEM((spread, 2 * nb, 128), F32),
            pltpu.VMEM((spread, nb // 2, rank, 128), F32),
            pltpu.SemaphoreType.DMA((6,)),
            pltpu.SemaphoreType.DMA((CHUNKS, 2, 3)),
            pltpu.SemaphoreType.DMA((CHUNKS, 2, 3)),
            pltpu.SemaphoreType.DMA((spread,)),
            pltpu.SemaphoreType.DMA((spread,)),
            pltpu.SemaphoreType.DMA((spread,)),
            pltpu.SemaphoreType.DMA((spread,)),
        ],
        compiler_params=pltpu.CompilerParams(
            collective_id=0, has_side_effects=True, vmem_limit_bytes=LIMIT),
        name="exchange",
    )(*(pltpu.with_memory_space_constraint(x, pltpu.HBM) for x in (bins, snapshots, old_basis)))
    fresh, coherence = pl.pallas_call(
        update,
        out_shape=(
            jax.ShapeDtypeStruct(old_basis.shape, BF),
            jax.ShapeDtypeStruct((nb, 2, rank, rank), F32),
        ),
        in_specs=[smem, vmem, vmem, vmem, vmem, hbm],
        out_specs=(hbm, vmem),
        scratch_shapes=[
            pltpu.VMEM((nb * rows, points), BF),
            pltpu.VMEM((nb * rows, points), BF),
            pltpu.SemaphoreType.DMA((CHUNKS,)),
            pltpu.SemaphoreType.DMA((CHUNKS,)),
        ],
        compiler_params=pltpu.CompilerParams(vmem_limit_bytes=40 * 2**20),
        name="update",
    )(block_count, eigenvalues, coef, gram, spec, old_basis)
    return fresh, coherence


def solution(mesh):
    groups, spread = mesh.shape["ta"], mesh.shape["sa"]
    return jax.shard_map(
        functools.partial(local, groups, spread),
        mesh=mesh,
        in_specs=(P("ta", None, "sa"), P(), P("ta", None), P("ta", None, None, None, "sa"), P()),
        out_specs=(P("ta", None, None, None, "sa"), P("ta", None, None, None)),
        check_vma=False,
    )
```

```python
import functools
import math

import jax
import jax.numpy as jnp
from jax import lax
from jax.experimental import pallas as pl
from jax.experimental.pallas import tpu as pltpu
from jax.sharding import PartitionSpec as P

MESH = pl.DeviceIdType.MESH
BF = jnp.bfloat16
F32 = jnp.float32
CHUNKS = 8
LIMIT = 40 * 2**20


def dot_nt(a, b):
    return lax.dot_general(a, b, (((1,), (1,)), ((), ())), preferred_element_type=F32)


def split(x):
    high = x.astype(BF)
    return high, (x - high.astype(F32)).astype(BF)


def split3(x):
    high = x.astype(BF)
    rest = x - high.astype(F32)
    mid = rest.astype(BF)
    return high, mid, (rest - mid.astype(F32)).astype(BF)


def right_pick(x, pick):
    n = x.shape[0]
    out = jnp.dot(jnp.concatenate(split3(x), axis=0), pick, preferred_element_type=F32)
    return out[:n] + out[n:2 * n] + out[2 * n:]


def iota(shape, axis):
    return lax.broadcasted_iota(jnp.int32, shape, axis)


def div(x, n):
    assert n & (n - 1) == 0
    return lax.shift_right_logical(x, jnp.full(x.shape, n.bit_length() - 1, x.dtype))


def mod(x, n):
    assert n & (n - 1) == 0
    return jnp.bitwise_and(x, n - 1)


def ones_where(mask):
    return jnp.where(mask, 1.0, 0.0).astype(BF)


def exchange(groups, spread, bins_ref, snap_ref, basis_ref, spec_ref, coef_ref, gram_ref, ub,
             bins, xs, terms, recv, fwd, cbuf, gbuf, in_sem, b_sem, rs_send, rs_recv, g_send, g_recv, c_send, c_recv):
    assert groups == 4
    slice_len = snap_ref.shape[0]
    points = snap_ref.shape[2]
    nb, _, rank = basis_ref.shape[:3]
    nbins = bins_ref.shape[0]
    rows = 4 * rank
    step = points // CHUNKS
    total = slice_len * groups
    me_t = lax.axis_index("ta")
    me_s = lax.axis_index("sa")
    load_bins = pltpu.make_async_copy(bins_ref, bins, b_sem.at[2 * nb])
    load_bins.start()
    parts = [pl.ds(k * step, step) for k in range(CHUNKS)]
    loads = [[pltpu.make_async_copy(snap_ref.at[:, v, p], xs.at[v, :, p], in_sem.at[v, k]) for v in range(2)]
             for k, p in enumerate(parts)]
    for pair in loads:
        for load in pair:
            load.start()
    flat = basis_ref.reshape(nb * rows, points)
    halves = [pl.ds(h * 2 * rank, 2 * rank) for h in range(2 * nb)]
    load_basis = [pltpu.make_async_copy(flat.at[h], ub.at[h], b_sem.at[i]) for i, h in enumerate(halves)]

    near = me_t + 1 - 2 * lax.rem(me_t, 2)
    far = lax.rem(me_t + 2, 4)
    diagonal = lax.rem(near + 2, 4)
    barrier = pltpu.get_barrier_semaphore()
    for peer in (near, far):
        pl.semaphore_signal(barrier, inc=1, device_id=(peer, me_s), device_id_type=MESH)
    for d in range(1, spread):
        pl.semaphore_signal(barrier, inc=1, device_id=(me_t, lax.rem(me_s + d, spread)), device_id_type=MESH)

    t = iota((2 * nbins, slice_len), 1) + me_t * slice_len
    row = iota((2 * nbins, slice_len), 0)
    unit = 2.0 * math.pi / total
    window = (0.5 - 0.5 * jnp.cos(unit * t[:8].astype(F32))) * math.sqrt(8.0 / (3.0 * total))
    window = jnp.concatenate([window] * (2 * nbins // 8), axis=0)
    load_bins.wait()
    bin_of = jnp.zeros((2 * nbins, slice_len), jnp.int32)
    for b in range(nbins):
        bin_of = jnp.where(div(row, 2) == b, bins[b], bin_of)
    phase = jnp.bitwise_and(bin_of * t + mod(row, 2) * (total // 4), total - 1)
    th, tl = split(jnp.cos(unit * phase.astype(F32)) * window)
    left = jnp.concatenate(
        [jnp.concatenate([th, th], axis=1), jnp.concatenate([tl, jnp.zeros_like(tl)], axis=1)], axis=0)

    pl.semaphore_wait(barrier, 2 + spread - 1)

    def rs_copy(src, slot, v, k, peer):
        cols = pl.ds(k * step, step)
        return pltpu.make_async_remote_copy(
            src_ref=src.at[v, :, cols], dst_ref=recv.at[slot, v, :, cols],
            send_sem=rs_send.at[k, v, slot], recv_sem=rs_recv.at[k, v, slot],
            device_id=(peer, me_s), device_id_type=MESH)

    first, second = (near, far), (far, near)
    copies = {}
    for k in range(CHUNKS):
        cols = parts[k]
        for v in range(2):
            loads[k][v].wait()
            xh, xl = split(xs[v, :, cols])
            out = jnp.dot(left, jnp.concatenate([xh, xl], axis=0), preferred_element_type=F32)
            out = out[: 2 * nbins] + out[2 * nbins:]
            terms[:, v, :, cols] = out.reshape(groups, 2 * nb, step)
            copies[k, v, 0] = rs_copy(terms.at[diagonal], 0, v, k, first[v])
            copies[k, v, 1] = rs_copy(terms.at[first[v]], 1, v, k, first[v])
            copies[k, v, 0].start()
            copies[k, v, 1].start()
        if k == 1:
            for load in load_basis:
                load.start()

    def pass_on(k):
        cols = pl.ds(k * step, step)
        for v in range(2):
            copies[k, v, 0].wait_recv()
            fwd[v, :, cols] = terms[second[v], v, :, cols] + recv[0, v, :, cols]
            copies[k, v, 2] = rs_copy(fwd, 2, v, k, second[v])
            copies[k, v, 2].start()

    two = 2 * rows
    ri, ci = iota((two, two), 0), iota((two, two), 1)
    same_v = mod(ri, 2) + 2 * div(ri, rows) == mod(ci, 2) + 2 * div(ci, rows)
    r_c, c_c = mod(div(ri, 2 * rank), 2), mod(div(ci, 2 * rank), 2)
    keep_re = jnp.where(jnp.logical_and(same_v, r_c == c_c), 1.0, 0.0)
    keep_im = jnp.where(jnp.logical_and(same_v, r_c != c_c), jnp.where(r_c == 0, 1.0, -1.0), 0.0)
    pr, pc = iota((2 * two, 128), 0), iota((2 * two, 128), 1)
    place = ones_where(pc == mod(div(pr, 2), rank) + 2 * rank * mod(div(pr, rows), 2) + rank * div(pr, two))
    fold = ones_where(iota((rank, 3 * two), 0) == mod(div(iota((rank, 3 * two), 1), 2), rank))
    for p in range(nb // 2):
        for load in load_basis[4 * p:4 * p + 4]:
            load.wait()
        w = ub[pl.ds(p * two, two), :]
        big = dot_nt(w, w)
        for k in range(p * CHUNKS // nb, (p + 1) * CHUNKS // nb):
            pass_on(k)
        wide = right_pick(jnp.concatenate([big * keep_re, big * keep_im], axis=1), place)
        gbuf[me_s, p] = jnp.dot(fold, jnp.concatenate(split3(wide), axis=0), preferred_element_type=F32)
    g_copies = []
    for d in range(1, spread):
        copy = pltpu.make_async_remote_copy(
            src_ref=gbuf.at[me_s], dst_ref=gbuf.at[me_s], send_sem=g_send.at[d], recv_sem=g_recv.at[d],
            device_id=(me_t, lax.rem(me_s + d, spread)), device_id_type=MESH)
        copy.start()
        g_copies.append(copy)
    for k in range((nb // 2) * CHUNKS // nb, CHUNKS):
        pass_on(k)

    er, ec = iota((nb * rows, 128), 0), iota((nb * rows, 128), 1)
    pick = ones_where(mod(div(er, 2), rank) == ec)
    acc = jnp.zeros((8 * nb, nb * rows), F32)
    square = jnp.zeros((2 * nb, 128), F32)
    for k in range(CHUNKS):
        cols = pl.ds(k * step, step)
        for v in range(2):
            copies[k, v, 1].wait_recv()
            copies[k, v, 2].wait_recv()
        spec = terms[me_t, :, :, cols] + recv[1, :, :, cols] + recv[2, :, :, cols]
        sq = spec[0] * spec[0] + spec[1] * spec[1]
        for i in range(step // 128):
            square = square + sq[:, i * 128:(i + 1) * 128]
        both = jnp.concatenate(split(spec.reshape(4 * nb, step)), axis=0)
        spec_ref[:, cols] = both
        acc = acc + dot_nt(both, ub[:, cols])
    acc = acc[: 4 * nb] + acc[4 * nb:]
    ar, ac = iota((2 * nb, nb * rows), 0), iota((2 * nb, nb * rows), 1)
    acc = jnp.where(mod(ac, 2) == 0, acc[: 2 * nb], acc[2 * nb:])
    even = mod(ar, 2) == 0
    other = jnp.where(even, pltpu.roll(acc, 2 * nb - 1, 0), -pltpu.roll(acc, 1, 0))
    acc = jnp.where(mod(div(ac, 2 * rank), 2) == 0, acc, other)
    coef = right_pick(jnp.where(div(ar, 2) == div(ac, rows), acc, 0.0), pick)
    norm = jnp.sum(square, axis=1, keepdims=True)
    cbuf[me_s] = jnp.where(iota((2 * nb, 128), 1) == rank, norm, coef)
    c_copies = []
    for d in range(1, spread):
        copy = pltpu.make_async_remote_copy(
            src_ref=cbuf.at[me_s], dst_ref=cbuf.at[me_s], send_sem=c_send.at[d], recv_sem=c_recv.at[d],
            device_id=(me_t, lax.rem(me_s + d, spread)), device_id_type=MESH)
        copy.start()
        c_copies.append(copy)
    for copy in g_copies:
        copy.wait_recv()
    gram = gbuf[0]
    for s in range(1, spread):
        gram = gram + gbuf[s]
    gram_ref[...] = gram
    for copy in list(copies.values()) + g_copies:
        copy.wait_send()
    for copy in c_copies:
        copy.wait_recv()
    coef = cbuf[0]
    for s in range(1, spread):
        coef = coef + cbuf[s]
    coef_ref[...] = coef
    for copy in c_copies:
        copy.wait_send()


def update(count_ref, eig_ref, coef_ref, gram_ref, spec_ref, ub, fresh_ref, coh_ref, ob, out_sem):
    nb, _, rank = fresh_ref.shape[:3]
    points = fresh_ref.shape[4]
    rows = 4 * rank
    flat_out = fresh_ref.reshape(nb * rows, points)
    halves = [pl.ds(h * 2 * rank, 2 * rank) for h in range(2 * nb)]
    stores = [pltpu.make_async_copy(ob.at[h], flat_out.at[h], out_sem.at[i]) for i, h in enumerate(halves)]
    count = jnp.full((1, 1), count_ref[0], jnp.int32).astype(F32)
    w_old = count / (count + 1.0)
    w_new = 1.0 / (count + 1.0)
    scaled = w_old * eig_ref[...]
    coef = coef_ref[...]
    coef_t = jnp.transpose(coef)
    scaled_t = jnp.transpose(jnp.concatenate([scaled, scaled], axis=0))
    eye = iota((rank, rank), 0) == iota((rank, rank), 1)
    r8 = iota((2 * nb, 128), 0)
    k_p = jnp.zeros((2 * nb, 128), F32)
    k_s = jnp.zeros((2 * nb, 128), F32)
    k_a = jnp.zeros((2 * nb, 128), F32)
    pad = jnp.zeros((1, 128 - rank), F32)
    for b in range(nb):
        g = gram_ref[b // 2]
        at = 2 * rank * (b % 2)
        g_re, g_im = g[:, at:at + rank], g[:, at + rank:at + 2 * rank]
        cr, ci = coef[2 * b:2 * b + 1, :rank], coef[2 * b + 1:2 * b + 2, :rank]
        cr_c, ci_c = coef_t[:rank, 2 * b:2 * b + 1], coef_t[:rank, 2 * b + 1:2 * b + 2]
        norm = coef[2 * b:2 * b + 1, rank:rank + 1] + coef[2 * b + 1:2 * b + 2, rank:rank + 1]
        a, a_c = scaled[b:b + 1], scaled_t[:, b:b + 1]
        weight = w_new * (a_c + a) + (w_new * w_new) * norm
        pair = a_c * a
        full_re = pair * g_re + weight * (cr_c * cr + ci_c * ci)
        full_im = pair * g_im + weight * (ci_c * cr - cr_c * ci)
        diag = jnp.where(eye, full_re, 0.0)
        inv = 1.0 / jnp.sqrt(jnp.sum(diag, axis=0, keepdims=True) + 1e-06)
        inv_c = 1.0 / jnp.sqrt(jnp.sum(diag, axis=1, keepdims=True) + 1e-06)
        outer = inv_c * inv
        coh_ref[b, 0] = full_re * outer
        coh_ref[b, 1] = full_im * outer
        p_row = jnp.concatenate([inv * w_new * cr, pad], axis=1)
        q_row = jnp.concatenate([inv * w_new * ci, pad], axis=1)
        a_row = jnp.concatenate([inv * a, pad], axis=1)
        k_p = jnp.where(r8 == 2 * b, p_row, jnp.where(r8 == 2 * b + 1, q_row, k_p))
        k_s = jnp.where(r8 == 2 * b, -q_row, jnp.where(r8 == 2 * b + 1, p_row, k_s))
        k_a = jnp.where(r8 == 2 * b, a_row, k_a)
    wide = 12 * nb
    lane = iota((2 * nb, 128), 1)
    k_mix = jnp.where(lane < rank, k_p, pltpu.roll(k_s, rank, 1))
    k_gain = jnp.where(lane < rank, k_a, pltpu.roll(k_a, rank, 1))
    er, ec = iota((nb * rows, 128), 0), iota((nb * rows, 128), 1)
    pick = ones_where(mod(div(er, 2), 2 * rank) == ec)
    values = jnp.concatenate([k_mix] * 6 + [k_gain], axis=0)
    spread_out = dot_nt(jnp.concatenate([pick] * 3, axis=1), jnp.concatenate(split3(values), axis=1))
    rr, rc = iota(spread_out.shape, 0), iota(spread_out.shape, 1)
    match = div(rr, rows) == mod(div(rc, 2), nb)
    gain = jnp.sum(jnp.where(jnp.logical_and(match, jnp.logical_and(rc >= wide, mod(rc, 2) == 0)), spread_out, 0.0),
                   axis=1, keepdims=True)
    match = jnp.logical_and(match, mod(rr, 2) == mod(div(rc, 2 * nb), 2))
    mix = jnp.where(match, spread_out, 0.0)[:, :wide]
    mh = mix.astype(BF).astype(F32)
    left = jnp.where(rc[:, :wide] < 8 * nb, mh, mix - mh).astype(BF)
    step = 512
    for i, h in enumerate(halves):
        at = i * 2 * rank
        lh, gh = left[at:at + 2 * rank], gain[at:at + 2 * rank]
        for k in range(points // step):
            cols = pl.ds(k * step, step)
            right = jnp.concatenate([spec_ref[:, cols], spec_ref[: 4 * nb, cols]], axis=0)
            add = jnp.dot(lh, right, preferred_element_type=F32)
            ob[h, cols] = (gh * ub[h, cols].astype(F32) + add).astype(BF)
        stores[i].start()
    for store in stores:
        store.wait()


def local(groups, spread, snapshots, bins, eigenvalues, old_basis, block_count):
    slice_len, _, points = snapshots.shape
    nb, _, rank = old_basis.shape[:3]
    rows = 4 * rank
    vmem = pl.BlockSpec(memory_space=pltpu.VMEM)
    smem = pl.BlockSpec(memory_space=pltpu.SMEM)
    hbm = pl.BlockSpec(memory_space=pl.ANY)
    spec, coef, gram, flat = pl.pallas_call(
        functools.partial(exchange, groups, spread),
        out_shape=(
            jax.ShapeDtypeStruct((8 * nb, points), BF),
            jax.ShapeDtypeStruct((2 * nb, 128), F32),
            jax.ShapeDtypeStruct((nb // 2, rank, 128), F32),
            jax.ShapeDtypeStruct((nb * rows, points), BF),
        ),
        in_specs=[pl.BlockSpec(memory_space=pltpu.HBM)] * 3,
        out_specs=(vmem, vmem, vmem, vmem),
        scratch_shapes=[
            pltpu.SMEM(bins.shape, jnp.int32),
            pltpu.VMEM((2, slice_len, points), F32),
            pltpu.VMEM((groups, 2, 2 * nb, points), F32),
            pltpu.VMEM((3, 2, 2 * nb, points), F32),
            pltpu.VMEM((2, 2 * nb, points), F32),
            pltpu.VMEM((spread, 2 * nb, 128), F32),
            pltpu.VMEM((spread, nb // 2, rank, 128), F32),
            pltpu.SemaphoreType.DMA((2, CHUNKS)),
            pltpu.SemaphoreType.DMA((2 * nb + 1,)),
            pltpu.SemaphoreType.DMA((CHUNKS, 2, 3)),
            pltpu.SemaphoreType.DMA((CHUNKS, 2, 3)),
            pltpu.SemaphoreType.DMA((spread,)),
            pltpu.SemaphoreType.DMA((spread,)),
            pltpu.SemaphoreType.DMA((spread,)),
            pltpu.SemaphoreType.DMA((spread,)),
        ],
        compiler_params=pltpu.CompilerParams(
            collective_id=0, has_side_effects=True, vmem_limit_bytes=LIMIT),
        name="exchange",
    )(*(pltpu.with_memory_space_constraint(x, pltpu.HBM) for x in (bins, snapshots, old_basis)))
    fresh, coherence = pl.pallas_call(
        update,
        out_shape=(
            jax.ShapeDtypeStruct(old_basis.shape, BF),
            jax.ShapeDtypeStruct((nb, 2, rank, rank), F32),
        ),
        in_specs=[smem, vmem, vmem, vmem, vmem, vmem],
        out_specs=(hbm, vmem),
        scratch_shapes=[
            pltpu.VMEM((nb * rows, points), BF),
            pltpu.SemaphoreType.DMA((2 * nb,)),
        ],
        compiler_params=pltpu.CompilerParams(vmem_limit_bytes=40 * 2**20),
        name="update",
    )(block_count, eigenvalues, coef, gram, spec, flat)
    return fresh, coherence


def solution(mesh):
    groups, spread = mesh.shape["ta"], mesh.shape["sa"]
    return jax.shard_map(
        functools.partial(local, groups, spread),
        mesh=mesh,
        in_specs=(P("ta", None, "sa"), P(), P("ta", None), P("ta", None, None, None, "sa"), P()),
        out_specs=(P("ta", None, None, None, "sa"), P("ta", None, None, None)),
        check_vma=False,
    )
```

```python
import functools
import math

import jax
import jax.numpy as jnp
from jax import lax
from jax.experimental import pallas as pl
from jax.experimental.pallas import tpu as pltpu
from jax.sharding import PartitionSpec as P

MESH = pl.DeviceIdType.MESH
BF = jnp.bfloat16
F32 = jnp.float32
CHUNKS = 8
LIMIT = 40 * 2**20


def dot_nt(a, b):
    return lax.dot_general(a, b, (((1,), (1,)), ((), ())), preferred_element_type=F32)


def split(x):
    high = x.astype(BF)
    return high, (x - high.astype(F32)).astype(BF)


def split3(x):
    high = x.astype(BF)
    rest = x - high.astype(F32)
    mid = rest.astype(BF)
    return high, mid, (rest - mid.astype(F32)).astype(BF)


def right_pick(x, pick):
    n = x.shape[0]
    out = jnp.dot(jnp.concatenate(split3(x), axis=0), pick, preferred_element_type=F32)
    return out[:n] + out[n:2 * n] + out[2 * n:]


def iota(shape, axis):
    return lax.broadcasted_iota(jnp.int32, shape, axis)


def div(x, n):
    assert n & (n - 1) == 0
    return lax.shift_right_logical(x, jnp.full(x.shape, n.bit_length() - 1, x.dtype))


def mod(x, n):
    assert n & (n - 1) == 0
    return jnp.bitwise_and(x, n - 1)


def ones_where(mask):
    return jnp.where(mask, 1.0, 0.0).astype(BF)


def exchange(groups, spread, bins_ref, snap_ref, basis_ref, spec_ref, coef_ref, gram_ref, ub,
             bins, xs, terms, recv, fwd, cbuf, gsum, gbuf, in_sem, b_sem, rs_send, rs_recv, g_send, g_recv, h_send, h_recv, c_send, c_recv):
    assert groups == 4
    slice_len = snap_ref.shape[0]
    points = snap_ref.shape[2]
    nb, _, rank = basis_ref.shape[:3]
    nbins = bins_ref.shape[0]
    rows = 4 * rank
    step = points // CHUNKS
    total = slice_len * groups
    me_t = lax.axis_index("ta")
    me_s = lax.axis_index("sa")
    load_bins = pltpu.make_async_copy(bins_ref, bins, b_sem.at[2 * nb])
    load_bins.start()
    parts = [pl.ds(k * step, step) for k in range(CHUNKS)]
    loads = [[pltpu.make_async_copy(snap_ref.at[:, v, p], xs.at[v, :, p], in_sem.at[v, k]) for v in range(2)]
             for k, p in enumerate(parts)]
    for pair in loads:
        for load in pair:
            load.start()
    flat = basis_ref.reshape(nb * rows, points)
    halves = [pl.ds(h * 2 * rank, 2 * rank) for h in range(2 * nb)]
    load_basis = [pltpu.make_async_copy(flat.at[h], ub.at[h], b_sem.at[i]) for i, h in enumerate(halves)]

    near = me_t + 1 - 2 * lax.rem(me_t, 2)
    far = lax.rem(me_t + 2, 4)
    diagonal = lax.rem(near + 2, 4)
    barrier = pltpu.get_barrier_semaphore()
    for peer in (near, far):
        pl.semaphore_signal(barrier, inc=1, device_id=(peer, me_s), device_id_type=MESH)
    for d in range(1, spread):
        pl.semaphore_signal(barrier, inc=1, device_id=(me_t, lax.rem(me_s + d, spread)), device_id_type=MESH)

    t = iota((2 * nbins, slice_len), 1) + me_t * slice_len
    row = iota((2 * nbins, slice_len), 0)
    unit = 2.0 * math.pi / total
    window = (0.5 - 0.5 * jnp.cos(unit * t[:8].astype(F32))) * math.sqrt(8.0 / (3.0 * total))
    window = jnp.concatenate([window] * (2 * nbins // 8), axis=0)
    load_bins.wait()
    bin_of = jnp.zeros((2 * nbins, slice_len), jnp.int32)
    for b in range(nbins):
        bin_of = jnp.where(div(row, 2) == b, bins[b], bin_of)
    phase = jnp.bitwise_and(bin_of * t + mod(row, 2) * (total // 4), total - 1)
    th, tl = split(jnp.cos(unit * phase.astype(F32)) * window)
    left = jnp.concatenate(
        [jnp.concatenate([th, th], axis=1), jnp.concatenate([tl, jnp.zeros_like(tl)], axis=1)], axis=0)

    pl.semaphore_wait(barrier, 2 + spread - 1)

    def rs_copy(src, slot, v, k, peer):
        cols = pl.ds(k * step, step)
        return pltpu.make_async_remote_copy(
            src_ref=src.at[v, :, cols], dst_ref=recv.at[slot, v, :, cols],
            send_sem=rs_send.at[k, v, slot], recv_sem=rs_recv.at[k, v, slot],
            device_id=(peer, me_s), device_id_type=MESH)

    first, second = (near, far), (far, near)
    copies = {}
    for k in range(CHUNKS):
        cols = parts[k]
        for v in range(2):
            loads[k][v].wait()
            xh, xl = split(xs[v, :, cols])
            out = jnp.dot(left, jnp.concatenate([xh, xl], axis=0), preferred_element_type=F32)
            out = out[: 2 * nbins] + out[2 * nbins:]
            terms[:, v, :, cols] = out.reshape(groups, 2 * nb, step)
            copies[k, v, 0] = rs_copy(terms.at[diagonal], 0, v, k, first[v])
            copies[k, v, 1] = rs_copy(terms.at[first[v]], 1, v, k, first[v])
            copies[k, v, 0].start()
            copies[k, v, 1].start()
        if k == 1:
            for load in load_basis:
                load.start()

    def pass_on(k):
        cols = pl.ds(k * step, step)
        for v in range(2):
            copies[k, v, 0].wait_recv()
            fwd[v, :, cols] = terms[second[v], v, :, cols] + recv[0, v, :, cols]
            copies[k, v, 2] = rs_copy(fwd, 2, v, k, second[v])
            copies[k, v, 2].start()

    two = 2 * rows
    ri, ci = iota((two, two), 0), iota((two, two), 1)
    same_v = mod(ri, 2) + 2 * div(ri, rows) == mod(ci, 2) + 2 * div(ci, rows)
    r_c, c_c = mod(div(ri, 2 * rank), 2), mod(div(ci, 2 * rank), 2)
    keep_re = jnp.where(jnp.logical_and(same_v, r_c == c_c), 1.0, 0.0)
    keep_im = jnp.where(jnp.logical_and(same_v, r_c != c_c), jnp.where(r_c == 0, 1.0, -1.0), 0.0)
    pr, pc = iota((2 * two, 128), 0), iota((2 * two, 128), 1)
    place = ones_where(pc == mod(div(pr, 2), rank) + 2 * rank * mod(div(pr, rows), 2) + rank * div(pr, two))
    fold = ones_where(iota((rank, 3 * two), 0) == mod(div(iota((rank, 3 * two), 1), 2), rank))
    late = CHUNKS // 2
    for k in range(late):
        pass_on(k)
    for p in range(nb // 2):
        for load in load_basis[4 * p:4 * p + 4]:
            load.wait()
        w = ub[pl.ds(p * two, two), :]
        big = dot_nt(w, w)
        for k in range(late + p * late // (nb // 2), late + (p + 1) * late // (nb // 2)):
            pass_on(k)
        wide = right_pick(jnp.concatenate([big * keep_re, big * keep_im], axis=1), place)
        gsum[p * rank:(p + 1) * rank] = jnp.dot(
            fold, jnp.concatenate(split3(wide), axis=0), preferred_element_type=F32)

    def to_all(src, dst, send_sem, recv_sem):
        out = []
        for d in range(1, spread):
            peer = lax.rem(me_s + d, spread)
            out.append(pltpu.make_async_remote_copy(
                src_ref=src(peer), dst_ref=dst, send_sem=send_sem.at[d], recv_sem=recv_sem.at[d],
                device_id=(me_t, peer), device_id_type=MESH))
            out[-1].start()
        return out

    g_rows = nb // 2 * rank
    share = g_rows // spread if g_rows % (8 * spread) == 0 else g_rows
    shared = share < g_rows

    def mine(device):
        return pl.ds(pl.multiple_of(device * share, 8), share) if shared else slice(None)

    g_copies = to_all(lambda peer: gsum.at[mine(peer)], gbuf.at[me_s], g_send, g_recv)

    def sum_gram():
        for copy in g_copies:
            copy.wait_recv()
        gbuf[me_s] = gsum[mine(me_s)]
        gram = gbuf[0]
        for s in range(1, spread):
            gram = gram + gbuf[s]
        gram_ref[mine(me_s)] = gram
        if not shared:
            return []
        return to_all(lambda peer: gram_ref.at[mine(me_s)], gram_ref.at[mine(me_s)], h_send, h_recv)

    er, ec = iota((nb * rows, 128), 0), iota((nb * rows, 128), 1)
    pick = ones_where(mod(div(er, 2), rank) == ec)
    acc = jnp.zeros((8 * nb, nb * rows), F32)
    square = jnp.zeros((2 * nb, 128), F32)
    for k in range(CHUNKS):
        if k == CHUNKS - 1:
            h_copies = sum_gram()
        cols = pl.ds(k * step, step)
        for v in range(2):
            copies[k, v, 1].wait_recv()
            copies[k, v, 2].wait_recv()
        spec = terms[me_t, :, :, cols] + recv[1, :, :, cols] + recv[2, :, :, cols]
        sq = spec[0] * spec[0] + spec[1] * spec[1]
        for i in range(step // 128):
            square = square + sq[:, i * 128:(i + 1) * 128]
        both = jnp.concatenate(split(spec.reshape(4 * nb, step)), axis=0)
        spec_ref[:, cols] = both
        acc = acc + dot_nt(both, ub[:, cols])
    acc = acc[: 4 * nb] + acc[4 * nb:]
    ar, ac = iota((2 * nb, nb * rows), 0), iota((2 * nb, nb * rows), 1)
    acc = jnp.where(mod(ac, 2) == 0, acc[: 2 * nb], acc[2 * nb:])
    even = mod(ar, 2) == 0
    other = jnp.where(even, pltpu.roll(acc, 2 * nb - 1, 0), -pltpu.roll(acc, 1, 0))
    acc = jnp.where(mod(div(ac, 2 * rank), 2) == 0, acc, other)
    coef = right_pick(jnp.where(div(ar, 2) == div(ac, rows), acc, 0.0), pick)
    norm = jnp.sum(square, axis=1, keepdims=True)
    cbuf[me_s] = jnp.where(iota((2 * nb, 128), 1) == rank, norm, coef)
    c_copies = to_all(lambda peer: cbuf.at[me_s], cbuf.at[me_s], c_send, c_recv)
    for copy in list(copies.values()) + g_copies:
        copy.wait_send()
    for copy in h_copies + c_copies:
        copy.wait_recv()
    coef = cbuf[0]
    for s in range(1, spread):
        coef = coef + cbuf[s]
    coef_ref[...] = coef
    for copy in h_copies + c_copies:
        copy.wait_send()


def update(count_ref, eig_ref, coef_ref, gram_ref, spec_ref, ub, fresh_ref, coh_ref, ob, out_sem):
    nb, _, rank = fresh_ref.shape[:3]
    points = fresh_ref.shape[4]
    rows = 4 * rank
    flat_out = fresh_ref.reshape(nb * rows, points)
    halves = [pl.ds(h * 2 * rank, 2 * rank) for h in range(2 * nb)]
    stores = [pltpu.make_async_copy(ob.at[h], flat_out.at[h], out_sem.at[i]) for i, h in enumerate(halves)]
    coef = coef_ref[...]
    count = count_ref[...].astype(F32)
    w_old = count / (count + 1.0)
    w_new = 1.0 / (count + 1.0)
    scaled = w_old * eig_ref[...]
    coef_t = jnp.transpose(coef)
    scaled_t = jnp.transpose(jnp.concatenate([scaled, scaled], axis=0))
    eye = iota((rank, rank), 0) == iota((rank, rank), 1)
    r8 = iota((2 * nb, 128), 0)
    k_p = jnp.zeros((2 * nb, 128), F32)
    k_s = jnp.zeros((2 * nb, 128), F32)
    k_a = jnp.zeros((2 * nb, 128), F32)
    pad = jnp.zeros((1, 128 - rank), F32)
    for b in range(nb):
        g = gram_ref[b // 2 * rank:(b // 2 + 1) * rank]
        at = 2 * rank * (b % 2)
        g_re, g_im = g[:, at:at + rank], g[:, at + rank:at + 2 * rank]
        cr, ci = coef[2 * b:2 * b + 1, :rank], coef[2 * b + 1:2 * b + 2, :rank]
        cr_c, ci_c = coef_t[:rank, 2 * b:2 * b + 1], coef_t[:rank, 2 * b + 1:2 * b + 2]
        norm = coef[2 * b:2 * b + 1, rank:rank + 1] + coef[2 * b + 1:2 * b + 2, rank:rank + 1]
        a, a_c = scaled[b:b + 1], scaled_t[:, b:b + 1]
        weight = w_new * (a_c + a) + (w_new * w_new) * norm
        pair = a_c * a
        full_re = pair * g_re + weight * (cr_c * cr + ci_c * ci)
        full_im = pair * g_im + weight * (ci_c * cr - cr_c * ci)
        diag = jnp.where(eye, full_re, 0.0)
        inv = 1.0 / jnp.sqrt(jnp.sum(diag, axis=0, keepdims=True) + 1e-06)
        inv_c = 1.0 / jnp.sqrt(jnp.sum(diag, axis=1, keepdims=True) + 1e-06)
        outer = inv_c * inv
        coh_ref[b, 0] = full_re * outer
        coh_ref[b, 1] = full_im * outer
        p_row = jnp.concatenate([inv * w_new * cr, pad], axis=1)
        q_row = jnp.concatenate([inv * w_new * ci, pad], axis=1)
        a_row = jnp.concatenate([inv * a, pad], axis=1)
        k_p = jnp.where(r8 == 2 * b, p_row, jnp.where(r8 == 2 * b + 1, q_row, k_p))
        k_s = jnp.where(r8 == 2 * b, -q_row, jnp.where(r8 == 2 * b + 1, p_row, k_s))
        k_a = jnp.where(r8 == 2 * b, a_row, k_a)
    wide = 12 * nb
    lane = iota((2 * nb, 128), 1)
    k_mix = jnp.where(lane < rank, k_p, pltpu.roll(k_s, rank, 1))
    k_gain = jnp.where(lane < rank, k_a, pltpu.roll(k_a, rank, 1))
    er, ec = iota((nb * rows, 128), 0), iota((nb * rows, 128), 1)
    pick = ones_where(mod(div(er, 2), 2 * rank) == ec)
    values = jnp.concatenate([k_mix] * 6 + [k_gain], axis=0)
    spread_out = dot_nt(jnp.concatenate([pick] * 3, axis=1), jnp.concatenate(split3(values), axis=1))
    rr, rc = iota(spread_out.shape, 0), iota(spread_out.shape, 1)
    match = div(rr, rows) == mod(div(rc, 2), nb)
    gain = jnp.sum(jnp.where(jnp.logical_and(match, jnp.logical_and(rc >= wide, mod(rc, 2) == 0)), spread_out, 0.0),
                   axis=1, keepdims=True)
    match = jnp.logical_and(match, mod(rr, 2) == mod(div(rc, 2 * nb), 2))
    mix = jnp.where(match, spread_out, 0.0)[:, :wide]
    mh = mix.astype(BF).astype(F32)
    left = jnp.where(rc[:, :wide] < 8 * nb, mh, mix - mh).astype(BF)
    step = 512
    for i, h in enumerate(halves):
        at = i * 2 * rank
        lh, gh = left[at:at + 2 * rank], gain[at:at + 2 * rank]
        for k in range(points // step):
            cols = pl.ds(k * step, step)
            right = jnp.concatenate([spec_ref[:, cols], spec_ref[: 4 * nb, cols]], axis=0)
            add = jnp.dot(lh, right, preferred_element_type=F32)
            ob[h, cols] = (gh * ub[h, cols].astype(F32) + add).astype(BF)
        stores[i].start()
    for store in stores:
        store.wait()


def local(groups, spread, snapshots, bins, eigenvalues, old_basis, block_count):
    slice_len, _, points = snapshots.shape
    nb, _, rank = old_basis.shape[:3]
    rows = 4 * rank
    g_rows = nb // 2 * rank
    share = g_rows // spread if g_rows % (8 * spread) == 0 else g_rows
    vmem = pl.BlockSpec(memory_space=pltpu.VMEM)
    hbm = pl.BlockSpec(memory_space=pl.ANY)
    spec, coef, gram, flat = pl.pallas_call(
        functools.partial(exchange, groups, spread),
        out_shape=(
            jax.ShapeDtypeStruct((8 * nb, points), BF),
            jax.ShapeDtypeStruct((2 * nb, 128), F32),
            jax.ShapeDtypeStruct((g_rows, 128), F32),
            jax.ShapeDtypeStruct((nb * rows, points), BF),
        ),
        in_specs=[pl.BlockSpec(memory_space=pltpu.HBM)] * 3,
        out_specs=(vmem, vmem, vmem, vmem),
        scratch_shapes=[
            pltpu.SMEM(bins.shape, jnp.int32),
            pltpu.VMEM((2, slice_len, points), F32),
            pltpu.VMEM((groups, 2, 2 * nb, points), F32),
            pltpu.VMEM((3, 2, 2 * nb, points), F32),
            pltpu.VMEM((2, 2 * nb, points), F32),
            pltpu.VMEM((spread, 2 * nb, 128), F32),
            pltpu.VMEM((g_rows, 128), F32),
            pltpu.VMEM((spread, share, 128), F32),
            pltpu.SemaphoreType.DMA((2, CHUNKS)),
            pltpu.SemaphoreType.DMA((2 * nb + 1,)),
            pltpu.SemaphoreType.DMA((CHUNKS, 2, 3)),
            pltpu.SemaphoreType.DMA((CHUNKS, 2, 3)),
            pltpu.SemaphoreType.DMA((spread,)),
            pltpu.SemaphoreType.DMA((spread,)),
            pltpu.SemaphoreType.DMA((spread,)),
            pltpu.SemaphoreType.DMA((spread,)),
            pltpu.SemaphoreType.DMA((spread,)),
            pltpu.SemaphoreType.DMA((spread,)),
        ],
        compiler_params=pltpu.CompilerParams(
            collective_id=0, has_side_effects=True, vmem_limit_bytes=LIMIT),
        name="exchange",
    )(*(pltpu.with_memory_space_constraint(x, pltpu.HBM) for x in (bins, snapshots, old_basis)))
    fresh, coherence = pl.pallas_call(
        update,
        out_shape=(
            jax.ShapeDtypeStruct(old_basis.shape, BF),
            jax.ShapeDtypeStruct((nb, 2, rank, rank), F32),
        ),
        in_specs=[vmem, vmem, vmem, vmem, vmem, vmem],
        out_specs=(hbm, vmem),
        scratch_shapes=[
            pltpu.VMEM((nb * rows, points), BF),
            pltpu.SemaphoreType.DMA((2 * nb,)),
        ],
        compiler_params=pltpu.CompilerParams(vmem_limit_bytes=40 * 2**20),
        name="update",
    )(block_count.reshape(1, 1), eigenvalues, coef, gram, spec, flat)
    return fresh, coherence


def solution(mesh):
    groups, spread = mesh.shape["ta"], mesh.shape["sa"]
    return jax.shard_map(
        functools.partial(local, groups, spread),
        mesh=mesh,
        in_specs=(P("ta", None, "sa"), P(), P("ta", None), P("ta", None, None, None, "sa"), P()),
        out_specs=(P("ta", None, None, None, "sa"), P("ta", None, None, None)),
        check_vma=False,
    )
```

```python
import functools
import math

import jax
import jax.numpy as jnp
from jax import lax
from jax.experimental import pallas as pl
from jax.experimental.pallas import tpu as pltpu
from jax.sharding import PartitionSpec as P

MESH = pl.DeviceIdType.MESH
BF = jnp.bfloat16
F32 = jnp.float32
CHUNKS = 4
LIMIT = 40 * 2**20


def dot_nt(a, b):
    return lax.dot_general(a, b, (((1,), (1,)), ((), ())), preferred_element_type=F32)


def split(x):
    high = x.astype(BF)
    return high, (x - high.astype(F32)).astype(BF)


def split3(x):
    high = x.astype(BF)
    rest = x - high.astype(F32)
    mid = rest.astype(BF)
    return high, mid, (rest - mid.astype(F32)).astype(BF)


def right_pick(x, pick):
    n = x.shape[0]
    out = jnp.dot(jnp.concatenate(split3(x), axis=0), pick, preferred_element_type=F32)
    return out[:n] + out[n:2 * n] + out[2 * n:]


def iota(shape, axis):
    return lax.broadcasted_iota(jnp.int32, shape, axis)


def div(x, n):
    assert n & (n - 1) == 0
    return lax.shift_right_logical(x, jnp.full(x.shape, n.bit_length() - 1, x.dtype))


def mod(x, n):
    assert n & (n - 1) == 0
    return jnp.bitwise_and(x, n - 1)


def ones_where(mask):
    return jnp.where(mask, 1.0, 0.0).astype(BF)


def exchange(groups, spread, bins_ref, snap_ref, basis_ref, spec_ref, coef_ref, gram_ref, ub,
             bins, xs, terms, recv, fwd, cbuf, gsum, gbuf, in_sem, b_sem, rs_send, rs_recv, sa_sem):
    assert groups == 4
    slice_len = snap_ref.shape[0]
    points = snap_ref.shape[2]
    nb, _, rank = basis_ref.shape[:3]
    nbins = bins_ref.shape[0]
    rows = 4 * rank
    step = points // CHUNKS
    total = slice_len * groups
    me_t = lax.axis_index("ta")
    me_s = lax.axis_index("sa")
    load_bins = pltpu.make_async_copy(bins_ref, bins, b_sem.at[nb // 2])
    load_bins.start()
    parts = [pl.ds(k * step, step) for k in range(CHUNKS)]
    flat_snap = snap_ref.reshape(2 * slice_len, points)
    loads = [pltpu.make_async_copy(flat_snap.at[:, p], xs.at[:, p], in_sem.at[k]) for k, p in enumerate(parts)]
    for load in loads:
        load.start()
    flat = basis_ref.reshape(nb * rows, points)
    pairs = [pl.ds(p * 2 * rows, 2 * rows) for p in range(nb // 2)]
    load_basis = [pltpu.make_async_copy(flat.at[h], ub.at[h], b_sem.at[i]) for i, h in enumerate(pairs)]

    near = me_t + 1 - 2 * lax.rem(me_t, 2)
    far = lax.rem(me_t + 2, 4)
    barrier = pltpu.get_barrier_semaphore()
    for peer in (near, far):
        pl.semaphore_signal(barrier, inc=1, device_id=(peer, me_s), device_id_type=MESH)
    for d in range(1, spread):
        pl.semaphore_signal(barrier, inc=1, device_id=(me_t, lax.rem(me_s + d, spread)), device_id_type=MESH)

    shape = (4 * nbins, 2 * slice_len)
    row, col = iota(shape, 0), iota(shape, 1)
    t = div(col, 2) + me_t * slice_len
    unit = 2.0 * math.pi / total
    window = (0.5 - 0.5 * jnp.cos(unit * t[:8].astype(F32))) * math.sqrt(8.0 / (3.0 * total))
    window = jnp.concatenate([window] * (4 * nbins // 8), axis=0)
    slot = mod(div(row, 2 * nb), 4)
    group = jnp.where(row < 2 * nbins, 2 * mod(slot, 2) + div(slot, 2), slot)
    index = group * nb + div(mod(row, 2 * nb), 2)
    load_bins.wait()
    bin_of = jnp.zeros(shape, jnp.int32)
    for b in range(nbins):
        bin_of = jnp.where(index == b, bins[b], bin_of)
    phase = jnp.bitwise_and(bin_of * t + mod(row, 2) * (total // 4), total - 1)
    table = jnp.cos(unit * phase.astype(F32)) * window
    th, tl = split(jnp.where(div(row, 2 * nbins) == mod(col, 2), table, 0.0))
    left = jnp.concatenate(
        [jnp.concatenate([th, th], axis=1), jnp.concatenate([tl, jnp.zeros_like(tl)], axis=1)], axis=0)

    pl.semaphore_wait(barrier, 2 + spread - 1)

    first, second = (near, far), (far, near)
    low, high = lax.rem(me_t, 2), me_t // 2
    out_pair = (2 * lax.rem(near, 2), 2 * (far // 2))
    own_slot = (2 * low + high, me_t)
    pass_slot = (2 * low + 1 - high, near)
    own_at, pass_at = (high, low), (1 - high, 1 - low)

    def step_one(v, cols, k):
        return pltpu.make_async_remote_copy(
            src_ref=terms.at[v, pl.ds(out_pair[v], 2), :, cols], dst_ref=recv.at[v, pl.ds(0, 2), :, cols],
            send_sem=rs_send.at[0, v], recv_sem=rs_recv.at[0, v, k],
            device_id=(first[v], me_s), device_id_type=MESH)

    def step_two(v, cols, k):
        return pltpu.make_async_remote_copy(
            src_ref=fwd.at[v, :, cols], dst_ref=recv.at[v, 2, :, cols],
            send_sem=rs_send.at[1, v], recv_sem=rs_recv.at[1, v, k],
            device_id=(second[v], me_s), device_id_type=MESH)

    for k, cols in enumerate(parts):
        loads[k].wait()
        out = jnp.dot(left, jnp.concatenate(split(xs[:, cols]), axis=0), preferred_element_type=F32)
        out = out[: 4 * nbins] + out[4 * nbins:]
        terms[:, :, :, cols] = out.reshape(2, groups, 2 * nb, step)
        for v in range(2):
            step_one(v, cols, k).start()
        if k == 0:
            for load in load_basis:
                load.start()

    def pass_on(k):
        cols = parts[k]
        for v in range(2):
            step_one(v, cols, k).wait_recv()
            fwd[v, :, cols] = terms[v, pass_slot[v], :, cols] + recv[v, pass_at[v], :, cols]
            step_two(v, cols, k).start()

    two = 2 * rows
    ri, ci = iota((two, two), 0), iota((two, two), 1)
    same_v = mod(ri, 2) + 2 * div(ri, rows) == mod(ci, 2) + 2 * div(ci, rows)
    r_c, c_c = mod(div(ri, 2 * rank), 2), mod(div(ci, 2 * rank), 2)
    keep_re = jnp.where(jnp.logical_and(same_v, r_c == c_c), 1.0, 0.0)
    keep_im = jnp.where(jnp.logical_and(same_v, r_c != c_c), jnp.where(r_c == 0, 1.0, -1.0), 0.0)
    pr, pc = iota((2 * two, 128), 0), iota((2 * two, 128), 1)
    place = ones_where(pc == mod(div(pr, 2), rank) + 2 * rank * mod(div(pr, rows), 2) + rank * div(pr, two))
    fold = ones_where(iota((rank, 3 * two), 0) == mod(div(iota((rank, 3 * two), 1), 2), rank))
    bigs = []
    for p in range(nb // 2):
        load_basis[p].wait()
        w = ub[pl.ds(p * two, two), :]
        bigs.append(dot_nt(w, w))
        for k in range(p * CHUNKS // (nb // 2), (p + 1) * CHUNKS // (nb // 2)):
            pass_on(k)
    for p, big in enumerate(bigs):
        wide = right_pick(jnp.concatenate([big * keep_re, big * keep_im], axis=1), place)
        gsum[p * rank:(p + 1) * rank] = jnp.dot(
            fold, jnp.concatenate(split3(wide), axis=0), preferred_element_type=F32)

    def to_all(src, dst, send_sem, recv_sem):
        for d in range(1, spread):
            peer = lax.rem(me_s + d, spread)
            pltpu.make_async_remote_copy(
                src_ref=src(peer), dst_ref=dst, send_sem=send_sem, recv_sem=recv_sem,
                device_id=(me_t, peer), device_id_type=MESH).start()

    def wait_all(like, sem):
        pltpu.make_async_copy(like, like, sem).wait()

    g_rows = nb // 2 * rank
    share = g_rows // spread if g_rows % (8 * spread) == 0 else g_rows
    shared = share < g_rows

    def mine(device):
        return pl.ds(pl.multiple_of(device * share, 8), share) if shared else slice(None)

    others = pl.ds(0, spread - 1)
    to_all(lambda peer: gsum.at[mine(peer)], gbuf.at[me_s], sa_sem.at[0], sa_sem.at[1])

    def sum_gram():
        wait_all(gbuf.at[others], sa_sem.at[1])
        gbuf[me_s] = gsum[mine(me_s)]
        gram = gbuf[0]
        for s in range(1, spread):
            gram = gram + gbuf[s]
        gram_ref[mine(me_s)] = gram
        if shared:
            to_all(lambda peer: gram_ref.at[mine(me_s)], gram_ref.at[mine(me_s)], sa_sem.at[2], sa_sem.at[3])

    er, ec = iota((nb * rows, 128), 0), iota((nb * rows, 128), 1)
    pick = ones_where(mod(div(er, 2), rank) == ec)
    acc = jnp.zeros((8 * nb, nb * rows), F32)
    square = jnp.zeros((2 * nb, 128), F32)
    for k, cols in enumerate(parts):
        if k == CHUNKS - 1:
            sum_gram()
        for v in range(2):
            step_two(v, cols, k).wait_recv()
        spec = jnp.stack([terms[v, own_slot[v], :, cols] + recv[v, own_at[v], :, cols] + recv[v, 2, :, cols]
                          for v in range(2)])
        sq = spec[0] * spec[0] + spec[1] * spec[1]
        for i in range(step // 128):
            square = square + sq[:, i * 128:(i + 1) * 128]
        both = jnp.concatenate(split(spec.reshape(4 * nb, step)), axis=0)
        spec_ref[:, cols] = both
        acc = acc + dot_nt(both, ub[:, cols])
    acc = acc[: 4 * nb] + acc[4 * nb:]
    ar, ac = iota((2 * nb, nb * rows), 0), iota((2 * nb, nb * rows), 1)
    acc = jnp.where(mod(ac, 2) == 0, acc[: 2 * nb], acc[2 * nb:])
    even = mod(ar, 2) == 0
    other = jnp.where(even, pltpu.roll(acc, 2 * nb - 1, 0), -pltpu.roll(acc, 1, 0))
    acc = jnp.where(mod(div(ac, 2 * rank), 2) == 0, acc, other)
    coef = right_pick(jnp.where(div(ar, 2) == div(ac, rows), acc, 0.0), pick)
    norm = jnp.sum(square, axis=1, keepdims=True)
    cbuf[me_s] = jnp.where(iota((2 * nb, 128), 1) == rank, norm, coef)
    to_all(lambda peer: cbuf.at[me_s], cbuf.at[me_s], sa_sem.at[4], sa_sem.at[5])
    every = pl.ds(0, points)
    for v in range(2):
        step_one(v, every, 0).wait_send()
        step_two(v, every, 0).wait_send()
    wait_all(gbuf.at[others], sa_sem.at[0])
    if shared:
        wait_all(gbuf.at[others], sa_sem.at[2])
        wait_all(gbuf.at[others], sa_sem.at[3])
    wait_all(cbuf.at[others], sa_sem.at[4])
    wait_all(cbuf.at[others], sa_sem.at[5])
    coef = cbuf[0]
    for s in range(1, spread):
        coef = coef + cbuf[s]
    coef_ref[...] = coef


def update(count_ref, eig_ref, coef_ref, gram_ref, spec_ref, ub, fresh_ref, coh_ref, ob, out_sem):
    nb, _, rank = fresh_ref.shape[:3]
    points = fresh_ref.shape[4]
    rows = 4 * rank
    flat_out = fresh_ref.reshape(nb * rows, points)
    halves = [pl.ds(h * 2 * rank, 2 * rank) for h in range(2 * nb)]
    stores = [pltpu.make_async_copy(ob.at[h], flat_out.at[h], out_sem.at[i]) for i, h in enumerate(halves)]
    coef = coef_ref[...]
    count = count_ref[...].astype(F32)
    w_old = count / (count + 1.0)
    w_new = 1.0 / (count + 1.0)
    scaled = w_old * eig_ref[...]
    coef_t = jnp.transpose(coef)
    scaled_t = jnp.transpose(jnp.concatenate([scaled, scaled], axis=0))
    eye = iota((rank, rank), 0) == iota((rank, rank), 1)
    r8 = iota((2 * nb, 128), 0)
    k_p = jnp.zeros((2 * nb, 128), F32)
    k_s = jnp.zeros((2 * nb, 128), F32)
    k_a = jnp.zeros((2 * nb, 128), F32)
    pad = jnp.zeros((1, 128 - rank), F32)
    for b in range(nb):
        g = gram_ref[b // 2 * rank:(b // 2 + 1) * rank]
        at = 2 * rank * (b % 2)
        g_re, g_im = g[:, at:at + rank], g[:, at + rank:at + 2 * rank]
        cr, ci = coef[2 * b:2 * b + 1, :rank], coef[2 * b + 1:2 * b + 2, :rank]
        cr_c, ci_c = coef_t[:rank, 2 * b:2 * b + 1], coef_t[:rank, 2 * b + 1:2 * b + 2]
        norm = coef[2 * b:2 * b + 1, rank:rank + 1] + coef[2 * b + 1:2 * b + 2, rank:rank + 1]
        a, a_c = scaled[b:b + 1], scaled_t[:, b:b + 1]
        weight = w_new * (a_c + a) + (w_new * w_new) * norm
        pair = a_c * a
        full_re = pair * g_re + weight * (cr_c * cr + ci_c * ci)
        full_im = pair * g_im + weight * (ci_c * cr - cr_c * ci)
        diag = jnp.where(eye, full_re, 0.0)
        inv = 1.0 / jnp.sqrt(jnp.sum(diag, axis=0, keepdims=True) + 1e-06)
        inv_c = 1.0 / jnp.sqrt(jnp.sum(diag, axis=1, keepdims=True) + 1e-06)
        outer = inv_c * inv
        coh_ref[b, 0] = full_re * outer
        coh_ref[b, 1] = full_im * outer
        p_row = jnp.concatenate([inv * w_new * cr, pad], axis=1)
        q_row = jnp.concatenate([inv * w_new * ci, pad], axis=1)
        a_row = jnp.concatenate([inv * a, pad], axis=1)
        k_p = jnp.where(r8 == 2 * b, p_row, jnp.where(r8 == 2 * b + 1, q_row, k_p))
        k_s = jnp.where(r8 == 2 * b, -q_row, jnp.where(r8 == 2 * b + 1, p_row, k_s))
        k_a = jnp.where(r8 == 2 * b, a_row, k_a)
    wide = 12 * nb
    lane = iota((2 * nb, 128), 1)
    k_mix = jnp.where(lane < rank, k_p, pltpu.roll(k_s, rank, 1))
    k_gain = jnp.where(lane < rank, k_a, pltpu.roll(k_a, rank, 1))
    er, ec = iota((nb * rows, 128), 0), iota((nb * rows, 128), 1)
    pick = ones_where(mod(div(er, 2), 2 * rank) == ec)
    values = jnp.concatenate([k_mix] * 6 + [k_gain], axis=0)
    spread_out = dot_nt(jnp.concatenate([pick] * 3, axis=1), jnp.concatenate(split3(values), axis=1))
    rr, rc = iota(spread_out.shape, 0), iota(spread_out.shape, 1)
    match = div(rr, rows) == mod(div(rc, 2), nb)
    gain = jnp.sum(jnp.where(jnp.logical_and(match, jnp.logical_and(rc >= wide, mod(rc, 2) == 0)), spread_out, 0.0),
                   axis=1, keepdims=True)
    match = jnp.logical_and(match, mod(rr, 2) == mod(div(rc, 2 * nb), 2))
    mix = jnp.where(match, spread_out, 0.0)[:, :wide]
    mh = mix.astype(BF).astype(F32)
    left = jnp.where(rc[:, :wide] < 8 * nb, mh, mix - mh).astype(BF)
    step = 512
    for i, h in enumerate(halves):
        at = i * 2 * rank
        lh, gh = left[at:at + 2 * rank], gain[at:at + 2 * rank]
        for k in range(points // step):
            cols = pl.ds(k * step, step)
            right = jnp.concatenate([spec_ref[:, cols], spec_ref[: 4 * nb, cols]], axis=0)
            add = jnp.dot(lh, right, preferred_element_type=F32)
            ob[h, cols] = (gh * ub[h, cols].astype(F32) + add).astype(BF)
        stores[i].start()
    for store in stores:
        store.wait()


def local(groups, spread, snapshots, bins, eigenvalues, old_basis, block_count):
    slice_len, _, points = snapshots.shape
    nb, _, rank = old_basis.shape[:3]
    rows = 4 * rank
    g_rows = nb // 2 * rank
    share = g_rows // spread if g_rows % (8 * spread) == 0 else g_rows
    vmem = pl.BlockSpec(memory_space=pltpu.VMEM)
    hbm = pl.BlockSpec(memory_space=pl.ANY)
    spec, coef, gram, flat = pl.pallas_call(
        functools.partial(exchange, groups, spread),
        out_shape=(
            jax.ShapeDtypeStruct((8 * nb, points), BF),
            jax.ShapeDtypeStruct((2 * nb, 128), F32),
            jax.ShapeDtypeStruct((g_rows, 128), F32),
            jax.ShapeDtypeStruct((nb * rows, points), BF),
        ),
        in_specs=[pl.BlockSpec(memory_space=pltpu.HBM)] * 3,
        out_specs=(vmem, vmem, vmem, vmem),
        scratch_shapes=[
            pltpu.SMEM(bins.shape, jnp.int32),
            pltpu.VMEM((2 * slice_len, points), F32),
            pltpu.VMEM((2, groups, 2 * nb, points), F32),
            pltpu.VMEM((2, 3, 2 * nb, points), F32),
            pltpu.VMEM((2, 2 * nb, points), F32),
            pltpu.VMEM((spread, 2 * nb, 128), F32),
            pltpu.VMEM((g_rows, 128), F32),
            pltpu.VMEM((spread, share, 128), F32),
            pltpu.SemaphoreType.DMA((CHUNKS,)),
            pltpu.SemaphoreType.DMA((nb // 2 + 1,)),
            pltpu.SemaphoreType.DMA((2, 2)),
            pltpu.SemaphoreType.DMA((2, 2, CHUNKS)),
            pltpu.SemaphoreType.DMA((6,)),
        ],
        compiler_params=pltpu.CompilerParams(
            collective_id=0, has_side_effects=True, vmem_limit_bytes=LIMIT),
        name="exchange",
    )(*(pltpu.with_memory_space_constraint(x, pltpu.HBM) for x in (bins, snapshots, old_basis)))
    fresh, coherence = pl.pallas_call(
        update,
        out_shape=(
            jax.ShapeDtypeStruct(old_basis.shape, BF),
            jax.ShapeDtypeStruct((nb, 2, rank, rank), F32),
        ),
        in_specs=[vmem, vmem, vmem, vmem, vmem, vmem],
        out_specs=(hbm, vmem),
        scratch_shapes=[
            pltpu.VMEM((nb * rows, points), BF),
            pltpu.SemaphoreType.DMA((2 * nb,)),
        ],
        compiler_params=pltpu.CompilerParams(vmem_limit_bytes=40 * 2**20),
        name="update",
    )(block_count.reshape(1, 1), eigenvalues, coef, gram, spec, flat)
    return fresh, coherence


def solution(mesh):
    groups, spread = mesh.shape["ta"], mesh.shape["sa"]
    return jax.shard_map(
        functools.partial(local, groups, spread),
        mesh=mesh,
        in_specs=(P("ta", None, "sa"), P(), P("ta", None), P("ta", None, None, None, "sa"), P()),
        out_specs=(P("ta", None, None, None, "sa"), P("ta", None, None, None)),
        check_vma=False,
    )
```

```python
import functools
import math

import jax
import jax.numpy as jnp
from jax import lax
from jax.experimental import pallas as pl
from jax.experimental.pallas import tpu as pltpu
from jax.sharding import PartitionSpec as P

MESH = pl.DeviceIdType.MESH
BF = jnp.bfloat16
F32 = jnp.float32
CHUNKS = 4
LIMIT = 40 * 2**20


def dot_nt(a, b):
    return lax.dot_general(a, b, (((1,), (1,)), ((), ())), preferred_element_type=F32)


def split(x):
    high = x.astype(BF)
    return high, (x - high.astype(F32)).astype(BF)


def split3(x):
    high = x.astype(BF)
    rest = x - high.astype(F32)
    mid = rest.astype(BF)
    return high, mid, (rest - mid.astype(F32)).astype(BF)


def right_pick(x, pick):
    n = x.shape[0]
    out = jnp.dot(jnp.concatenate(split3(x), axis=0), pick, preferred_element_type=F32)
    return out[:n] + out[n:2 * n] + out[2 * n:]


def iota(shape, axis):
    return lax.broadcasted_iota(jnp.int32, shape, axis)


def div(x, n):
    assert n & (n - 1) == 0
    return lax.shift_right_logical(x, jnp.full(x.shape, n.bit_length() - 1, x.dtype))


def mod(x, n):
    assert n & (n - 1) == 0
    return jnp.bitwise_and(x, n - 1)


def ones_where(mask):
    return jnp.where(mask, 1.0, 0.0).astype(BF)


def exchange(groups, spread, bins_ref, snap_ref, basis_ref, spec_ref, coef_ref, gram_ref, ub,
             bins, xs, terms, recv, fwd, cbuf, gbuf, in_sem, b_sem, rs_send, rs_recv, sa_sem):
    assert groups == 4
    slice_len = snap_ref.shape[0]
    points = snap_ref.shape[2]
    nb, _, rank = basis_ref.shape[:3]
    nbins = bins_ref.shape[0]
    rows = 4 * rank
    step = points // CHUNKS
    total = slice_len * groups
    me_t = lax.axis_index("ta")
    me_s = lax.axis_index("sa")
    load_bins = pltpu.make_async_copy(bins_ref, bins, b_sem.at[nb // 2])
    load_bins.start()
    parts = [pl.ds(k * step, step) for k in range(CHUNKS)]
    flat_snap = snap_ref.reshape(2 * slice_len, points)
    loads = [pltpu.make_async_copy(flat_snap.at[:, p], xs.at[:, p], in_sem.at[k]) for k, p in enumerate(parts)]
    for load in loads:
        load.start()
    flat = basis_ref.reshape(nb * rows, points)
    pairs = [pl.ds(p * 2 * rows, 2 * rows) for p in range(nb // 2)]
    load_basis = [pltpu.make_async_copy(flat.at[h], ub.at[h], b_sem.at[i]) for i, h in enumerate(pairs)]

    near = me_t + 1 - 2 * lax.rem(me_t, 2)
    far = lax.rem(me_t + 2, 4)
    barrier = pltpu.get_barrier_semaphore()
    for peer in (near, far):
        pl.semaphore_signal(barrier, inc=1, device_id=(peer, me_s), device_id_type=MESH)
    for d in range(1, spread):
        pl.semaphore_signal(barrier, inc=1, device_id=(me_t, lax.rem(me_s + d, spread)), device_id_type=MESH)

    shape = (4 * nbins, 2 * slice_len)
    row, col = iota(shape, 0), iota(shape, 1)
    t = div(col, 2) + me_t * slice_len
    unit = 2.0 * math.pi / total
    window = (0.5 - 0.5 * jnp.cos(unit * t[:8].astype(F32))) * math.sqrt(8.0 / (3.0 * total))
    window = jnp.concatenate([window] * (4 * nbins // 8), axis=0)
    slot = mod(div(row, 2 * nb), 4)
    group = jnp.where(row < 2 * nbins, 2 * mod(slot, 2) + div(slot, 2), slot)
    index = group * nb + div(mod(row, 2 * nb), 2)
    load_bins.wait()
    bin_of = jnp.zeros(shape, jnp.int32)
    for b in range(nbins):
        bin_of = jnp.where(index == b, bins[b], bin_of)
    phase = jnp.bitwise_and(bin_of * t + mod(row, 2) * (total // 4), total - 1)
    table = jnp.cos(unit * phase.astype(F32)) * window
    th, tl = split(jnp.where(div(row, 2 * nbins) == mod(col, 2), table, 0.0))
    left = jnp.concatenate(
        [jnp.concatenate([th, th], axis=1), jnp.concatenate([tl, jnp.zeros_like(tl)], axis=1)], axis=0)

    pl.semaphore_wait(barrier, 2 + spread - 1)

    first, second = (near, far), (far, near)
    low, high = lax.rem(me_t, 2), me_t // 2
    out_pair = (2 * lax.rem(near, 2), 2 * (far // 2))
    own_slot = (2 * low + high, me_t)
    pass_slot = (2 * low + 1 - high, near)
    own_at, pass_at = (high, low), (1 - high, 1 - low)

    def step_one(v, cols, k):
        return pltpu.make_async_remote_copy(
            src_ref=terms.at[v, pl.ds(out_pair[v], 2), :, cols], dst_ref=recv.at[v, pl.ds(0, 2), :, cols],
            send_sem=rs_send.at[0, v], recv_sem=rs_recv.at[0, v, k],
            device_id=(first[v], me_s), device_id_type=MESH)

    def step_two(v, cols, k):
        return pltpu.make_async_remote_copy(
            src_ref=fwd.at[v, :, cols], dst_ref=recv.at[v, 2, :, cols],
            send_sem=rs_send.at[1, v], recv_sem=rs_recv.at[1, v, k],
            device_id=(second[v], me_s), device_id_type=MESH)

    for k, cols in enumerate(parts):
        loads[k].wait()
        out = jnp.dot(left, jnp.concatenate(split(xs[:, cols]), axis=0), preferred_element_type=F32)
        out = out[: 4 * nbins] + out[4 * nbins:]
        terms[:, :, :, cols] = out.reshape(2, groups, 2 * nb, step)
        for v in range(2):
            step_one(v, cols, k).start()
        if k == 0:
            for load in load_basis:
                load.start()

    def pass_on(k):
        cols = parts[k]
        for v in range(2):
            step_one(v, cols, k).wait_recv()
            fwd[v, :, cols] = terms[v, pass_slot[v], :, cols] + recv[v, pass_at[v], :, cols]
            step_two(v, cols, k).start()

    two = 2 * rows
    ri, ci = iota((two, two), 0), iota((two, two), 1)
    same_v = mod(ri, 2) + 2 * div(ri, rows) == mod(ci, 2) + 2 * div(ci, rows)
    r_c, c_c = mod(div(ri, 2 * rank), 2), mod(div(ci, 2 * rank), 2)
    keep_re = jnp.where(jnp.logical_and(same_v, r_c == c_c), 1.0, 0.0)
    keep_im = jnp.where(jnp.logical_and(same_v, r_c != c_c), jnp.where(r_c == 0, 1.0, -1.0), 0.0)
    pr, pc = iota((2 * two, 128), 0), iota((2 * two, 128), 1)
    place = ones_where(pc == mod(div(pr, 2), rank) + 2 * rank * mod(div(pr, rows), 2) + rank * div(pr, two))
    fold = ones_where(iota((rank, 3 * two), 0) == mod(div(iota((rank, 3 * two), 1), 2), rank))
    bigs = []
    for p in range(nb // 2):
        load_basis[p].wait()
        w = ub[pl.ds(p * two, two), :]
        bigs.append(dot_nt(w, w))
        for k in range(p * CHUNKS // (nb // 2), (p + 1) * CHUNKS // (nb // 2)):
            pass_on(k)
    lane = iota((rank, 128), 1)
    upper = mod(lane, rank) >= iota((rank, 128), 0)
    packs = []
    for big in bigs:
        wide = right_pick(jnp.concatenate([big * keep_re, big * keep_im], axis=1), place)
        both = jnp.dot(fold, jnp.concatenate(split3(wide), axis=0), preferred_element_type=F32)
        packs.append(jnp.where(upper, both, pltpu.roll(both, 128 - rank, 1)))
    gbuf[me_s] = jnp.where(mod(lane, 2 * rank) < rank, packs[0], pltpu.roll(packs[1], rank, 1))

    def to_all(src, dst, send_sem, recv_sem):
        for d in range(1, spread):
            peer = lax.rem(me_s + d, spread)
            pltpu.make_async_remote_copy(
                src_ref=src(peer), dst_ref=dst, send_sem=send_sem, recv_sem=recv_sem,
                device_id=(me_t, peer), device_id_type=MESH).start()

    def wait_all(like, sem):
        pltpu.make_async_copy(like, like, sem).wait()

    others = pl.ds(0, spread - 1)
    to_all(lambda peer: gbuf.at[me_s], gbuf.at[me_s], sa_sem.at[0], sa_sem.at[1])

    er, ec = iota((nb * rows, 128), 0), iota((nb * rows, 128), 1)
    pick = ones_where(mod(div(er, 2), rank) == ec)
    acc = jnp.zeros((8 * nb, nb * rows), F32)
    square = jnp.zeros((2 * nb, 128), F32)
    for k, cols in enumerate(parts):
        for v in range(2):
            step_two(v, cols, k).wait_recv()
        spec = jnp.stack([terms[v, own_slot[v], :, cols] + recv[v, own_at[v], :, cols] + recv[v, 2, :, cols]
                          for v in range(2)])
        sq = spec[0] * spec[0] + spec[1] * spec[1]
        for i in range(step // 128):
            square = square + sq[:, i * 128:(i + 1) * 128]
        both = jnp.concatenate(split(spec.reshape(4 * nb, step)), axis=0)
        spec_ref[:, cols] = both
        acc = acc + dot_nt(both, ub[:, cols])
    acc = acc[: 4 * nb] + acc[4 * nb:]
    ar, ac = iota((2 * nb, nb * rows), 0), iota((2 * nb, nb * rows), 1)
    acc = jnp.where(mod(ac, 2) == 0, acc[: 2 * nb], acc[2 * nb:])
    even = mod(ar, 2) == 0
    other = jnp.where(even, pltpu.roll(acc, 2 * nb - 1, 0), -pltpu.roll(acc, 1, 0))
    acc = jnp.where(mod(div(ac, 2 * rank), 2) == 0, acc, other)
    coef = right_pick(jnp.where(div(ar, 2) == div(ac, rows), acc, 0.0), pick)
    norm = jnp.sum(square, axis=1, keepdims=True)
    cbuf[me_s] = jnp.where(iota((2 * nb, 128), 1) == rank, norm, coef)
    to_all(lambda peer: cbuf.at[me_s], cbuf.at[me_s], sa_sem.at[2], sa_sem.at[3])
    every = pl.ds(0, points)
    for v in range(2):
        step_one(v, every, 0).wait_send()
        step_two(v, every, 0).wait_send()
    wait_all(gbuf.at[others], sa_sem.at[0])
    wait_all(gbuf.at[others], sa_sem.at[1])
    gram = gbuf[0]
    for s in range(1, spread):
        gram = gram + gbuf[s]
    gram_ref[...] = gram
    wait_all(cbuf.at[others], sa_sem.at[2])
    wait_all(cbuf.at[others], sa_sem.at[3])
    coef = cbuf[0]
    for s in range(1, spread):
        coef = coef + cbuf[s]
    coef_ref[...] = coef


def update(count_ref, eig_ref, coef_ref, gram_ref, spec_ref, ub, fresh_ref, coh_ref, ob, out_sem):
    nb, _, rank = fresh_ref.shape[:3]
    points = fresh_ref.shape[4]
    rows = 4 * rank
    flat_out = fresh_ref.reshape(nb * rows, points)
    halves = [pl.ds(h * 2 * rank, 2 * rank) for h in range(2 * nb)]
    stores = [pltpu.make_async_copy(ob.at[h], flat_out.at[h], out_sem.at[i]) for i, h in enumerate(halves)]
    coef = coef_ref[...]
    count = count_ref[...].astype(F32)
    w_old = count / (count + 1.0)
    w_new = 1.0 / (count + 1.0)
    scaled = w_old * eig_ref[...]
    coef_t = jnp.transpose(coef)
    scaled_t = jnp.transpose(jnp.concatenate([scaled, scaled], axis=0))
    eye = iota((rank, rank), 0) == iota((rank, rank), 1)
    upper = iota((rank, rank), 0) <= iota((rank, rank), 1)
    lower = iota((rank, rank), 0) > iota((rank, rank), 1)
    gram = gram_ref[...]
    gram_t = jnp.transpose(gram)
    r8 = iota((2 * nb, 128), 0)
    k_p = jnp.zeros((2 * nb, 128), F32)
    k_s = jnp.zeros((2 * nb, 128), F32)
    k_a = jnp.zeros((2 * nb, 128), F32)
    pad = jnp.zeros((1, 128 - rank), F32)
    for b in range(nb):
        at = 2 * rank * (b % 2) + rank * (b // 2)
        g, g_t = gram[:, at:at + rank], gram_t[at:at + rank]
        g_re = jnp.where(upper, g, g_t)
        g_im = jnp.where(lower, g, jnp.where(eye, 0.0, -g_t))
        cr, ci = coef[2 * b:2 * b + 1, :rank], coef[2 * b + 1:2 * b + 2, :rank]
        cr_c, ci_c = coef_t[:rank, 2 * b:2 * b + 1], coef_t[:rank, 2 * b + 1:2 * b + 2]
        norm = coef[2 * b:2 * b + 1, rank:rank + 1] + coef[2 * b + 1:2 * b + 2, rank:rank + 1]
        a, a_c = scaled[b:b + 1], scaled_t[:, b:b + 1]
        weight = w_new * (a_c + a) + (w_new * w_new) * norm
        pair = a_c * a
        full_re = pair * g_re + weight * (cr_c * cr + ci_c * ci)
        full_im = pair * g_im + weight * (ci_c * cr - cr_c * ci)
        diag = jnp.where(eye, full_re, 0.0)
        inv = 1.0 / jnp.sqrt(jnp.sum(diag, axis=0, keepdims=True) + 1e-06)
        inv_c = 1.0 / jnp.sqrt(jnp.sum(diag, axis=1, keepdims=True) + 1e-06)
        outer = inv_c * inv
        coh_ref[b, 0] = full_re * outer
        coh_ref[b, 1] = full_im * outer
        p_row = jnp.concatenate([inv * w_new * cr, pad], axis=1)
        q_row = jnp.concatenate([inv * w_new * ci, pad], axis=1)
        a_row = jnp.concatenate([inv * a, pad], axis=1)
        k_p = jnp.where(r8 == 2 * b, p_row, jnp.where(r8 == 2 * b + 1, q_row, k_p))
        k_s = jnp.where(r8 == 2 * b, -q_row, jnp.where(r8 == 2 * b + 1, p_row, k_s))
        k_a = jnp.where(r8 == 2 * b, a_row, k_a)
    wide = 12 * nb
    lane = iota((2 * nb, 128), 1)
    k_mix = jnp.where(lane < rank, k_p, pltpu.roll(k_s, rank, 1))
    k_gain = jnp.where(lane < rank, k_a, pltpu.roll(k_a, rank, 1))
    er, ec = iota((nb * rows, 128), 0), iota((nb * rows, 128), 1)
    pick = ones_where(mod(div(er, 2), 2 * rank) == ec)
    values = jnp.concatenate([k_mix] * 6 + [k_gain], axis=0)
    spread_out = dot_nt(jnp.concatenate([pick] * 3, axis=1), jnp.concatenate(split3(values), axis=1))
    rr, rc = iota(spread_out.shape, 0), iota(spread_out.shape, 1)
    match = div(rr, rows) == mod(div(rc, 2), nb)
    gain = jnp.sum(jnp.where(jnp.logical_and(match, jnp.logical_and(rc >= wide, mod(rc, 2) == 0)), spread_out, 0.0),
                   axis=1, keepdims=True)
    match = jnp.logical_and(match, mod(rr, 2) == mod(div(rc, 2 * nb), 2))
    mix = jnp.where(match, spread_out, 0.0)[:, :wide]
    mh = mix.astype(BF).astype(F32)
    left = jnp.where(rc[:, :wide] < 8 * nb, mh, mix - mh).astype(BF)
    step = 512
    for i, h in enumerate(halves):
        at = i * 2 * rank
        lh, gh = left[at:at + 2 * rank], gain[at:at + 2 * rank]
        for k in range(points // step):
            cols = pl.ds(k * step, step)
            right = jnp.concatenate([spec_ref[:, cols], spec_ref[: 4 * nb, cols]], axis=0)
            add = jnp.dot(lh, right, preferred_element_type=F32)
            ob[h, cols] = (gh * ub[h, cols].astype(F32) + add).astype(BF)
        stores[i].start()
    for store in stores:
        store.wait()


def local(groups, spread, snapshots, bins, eigenvalues, old_basis, block_count):
    slice_len, _, points = snapshots.shape
    nb, _, rank = old_basis.shape[:3]
    rows = 4 * rank
    assert nb * rank == 128
    vmem = pl.BlockSpec(memory_space=pltpu.VMEM)
    hbm = pl.BlockSpec(memory_space=pl.ANY)
    spec, coef, gram, flat = pl.pallas_call(
        functools.partial(exchange, groups, spread),
        out_shape=(
            jax.ShapeDtypeStruct((8 * nb, points), BF),
            jax.ShapeDtypeStruct((2 * nb, 128), F32),
            jax.ShapeDtypeStruct((rank, 128), F32),
            jax.ShapeDtypeStruct((nb * rows, points), BF),
        ),
        in_specs=[pl.BlockSpec(memory_space=pltpu.HBM)] * 3,
        out_specs=(vmem, vmem, vmem, vmem),
        scratch_shapes=[
            pltpu.SMEM(bins.shape, jnp.int32),
            pltpu.VMEM((2 * slice_len, points), F32),
            pltpu.VMEM((2, groups, 2 * nb, points), F32),
            pltpu.VMEM((2, 3, 2 * nb, points), F32),
            pltpu.VMEM((2, 2 * nb, points), F32),
            pltpu.VMEM((spread, 2 * nb, 128), F32),
            pltpu.VMEM((spread, rank, 128), F32),
            pltpu.SemaphoreType.DMA((CHUNKS,)),
            pltpu.SemaphoreType.DMA((nb // 2 + 1,)),
            pltpu.SemaphoreType.DMA((2, 2)),
            pltpu.SemaphoreType.DMA((2, 2, CHUNKS)),
            pltpu.SemaphoreType.DMA((4,)),
        ],
        compiler_params=pltpu.CompilerParams(
            collective_id=0, has_side_effects=True, vmem_limit_bytes=LIMIT),
        name="exchange",
    )(*(pltpu.with_memory_space_constraint(x, pltpu.HBM) for x in (bins, snapshots, old_basis)))
    fresh, coherence = pl.pallas_call(
        update,
        out_shape=(
            jax.ShapeDtypeStruct(old_basis.shape, BF),
            jax.ShapeDtypeStruct((nb, 2, rank, rank), F32),
        ),
        in_specs=[vmem, vmem, vmem, vmem, vmem, vmem],
        out_specs=(hbm, vmem),
        scratch_shapes=[
            pltpu.VMEM((nb * rows, points), BF),
            pltpu.SemaphoreType.DMA((2 * nb,)),
        ],
        compiler_params=pltpu.CompilerParams(vmem_limit_bytes=40 * 2**20),
        name="update",
    )(block_count.reshape(1, 1), eigenvalues, coef, gram, spec, flat)
    return fresh, coherence


def solution(mesh):
    groups, spread = mesh.shape["ta"], mesh.shape["sa"]
    return jax.shard_map(
        functools.partial(local, groups, spread),
        mesh=mesh,
        in_specs=(P("ta", None, "sa"), P(), P("ta", None), P("ta", None, None, None, "sa"), P()),
        out_specs=(P("ta", None, None, None, "sa"), P("ta", None, None, None)),
        check_vma=False,
    )
```

```python
import functools
import math

import jax
import jax.numpy as jnp
from jax import lax
from jax.experimental import pallas as pl
from jax.experimental.pallas import tpu as pltpu
from jax.sharding import PartitionSpec as P

MESH = pl.DeviceIdType.MESH
BF = jnp.bfloat16
F32 = jnp.float32
CHUNKS = 8
LIMIT = 40 * 2**20


def dot_nt(a, b):
    return lax.dot_general(a, b, (((1,), (1,)), ((), ())), preferred_element_type=F32)


def split(x):
    high = x.astype(BF)
    return high, (x - high.astype(F32)).astype(BF)


def split3(x):
    high = x.astype(BF)
    rest = x - high.astype(F32)
    mid = rest.astype(BF)
    return high, mid, (rest - mid.astype(F32)).astype(BF)


def right_pick(x, pick):
    n = x.shape[0]
    out = jnp.dot(jnp.concatenate(split3(x), axis=0), pick, preferred_element_type=F32)
    return out[:n] + out[n:2 * n] + out[2 * n:]


def iota(shape, axis):
    return lax.broadcasted_iota(jnp.int32, shape, axis)


def div(x, n):
    assert n & (n - 1) == 0
    return lax.shift_right_logical(x, jnp.full(x.shape, n.bit_length() - 1, x.dtype))


def mod(x, n):
    assert n & (n - 1) == 0
    return jnp.bitwise_and(x, n - 1)


def ones_where(mask):
    return jnp.where(mask, 1.0, 0.0).astype(BF)


def exchange(groups, spread, bins_ref, snap_ref, basis_ref, spec_ref, coef_ref, gram_ref, ub,
             bins, xs, terms, recv, fwd, cbuf, gbuf, in_sem, b_sem, rs_send, rs_recv, sa_sem):
    assert groups == 4
    slice_len = snap_ref.shape[0]
    points = snap_ref.shape[2]
    nb, _, rank = basis_ref.shape[:3]
    nbins = bins_ref.shape[0]
    rows = 4 * rank
    step = points // CHUNKS
    total = slice_len * groups
    me_t = lax.axis_index("ta")
    me_s = lax.axis_index("sa")
    load_bins = pltpu.make_async_copy(bins_ref, bins, b_sem.at[nb // 2])
    load_bins.start()
    parts = [pl.ds(k * step, step) for k in range(CHUNKS)]
    flat_snap = snap_ref.reshape(2 * slice_len, points)
    loads = [pltpu.make_async_copy(flat_snap.at[:, p], xs.at[:, p], in_sem.at[k]) for k, p in enumerate(parts)]
    for load in loads:
        load.start()
    flat = basis_ref.reshape(nb * rows, points)
    pairs = [pl.ds(p * 2 * rows, 2 * rows) for p in range(nb // 2)]
    load_basis = [pltpu.make_async_copy(flat.at[h], ub.at[h], b_sem.at[i]) for i, h in enumerate(pairs)]

    near = me_t + 1 - 2 * lax.rem(me_t, 2)
    far = lax.rem(me_t + 2, 4)
    barrier = pltpu.get_barrier_semaphore()
    for peer in (near, far):
        pl.semaphore_signal(barrier, inc=1, device_id=(peer, me_s), device_id_type=MESH)
    for d in range(1, spread):
        pl.semaphore_signal(barrier, inc=1, device_id=(me_t, lax.rem(me_s + d, spread)), device_id_type=MESH)

    shape = (4 * nbins, 2 * slice_len)
    row, col = iota(shape, 0), iota(shape, 1)
    t = div(col, 2) + me_t * slice_len
    unit = 2.0 * math.pi / total
    window = (0.5 - 0.5 * jnp.cos(unit * t[:8].astype(F32))) * math.sqrt(8.0 / (3.0 * total))
    window = jnp.concatenate([window] * (4 * nbins // 8), axis=0)
    slot = mod(div(row, 2 * nb), 4)
    group = jnp.where(row < 2 * nbins, 2 * mod(slot, 2) + div(slot, 2), slot)
    index = group * nb + div(mod(row, 2 * nb), 2)
    load_bins.wait()
    bin_of = jnp.zeros(shape, jnp.int32)
    for b in range(nbins):
        bin_of = jnp.where(index == b, bins[b], bin_of)
    phase = jnp.bitwise_and(bin_of * t + mod(row, 2) * (total // 4), total - 1)
    table = jnp.cos(unit * phase.astype(F32)) * window
    th, tl = split(jnp.where(div(row, 2 * nbins) == mod(col, 2), table, 0.0))
    left = jnp.concatenate(
        [jnp.concatenate([th, th], axis=1), jnp.concatenate([tl, jnp.zeros_like(tl)], axis=1)], axis=0)

    pl.semaphore_wait(barrier, 2 + spread - 1)

    first, second = (near, far), (far, near)
    low, high = lax.rem(me_t, 2), me_t // 2
    out_pair = (2 * lax.rem(near, 2), 2 * (far // 2))
    own_slot = (2 * low + high, me_t)
    pass_slot = (2 * low + 1 - high, near)
    own_at, pass_at = (high, low), (1 - high, 1 - low)

    def step_one(v, cols, k):
        return pltpu.make_async_remote_copy(
            src_ref=terms.at[v, pl.ds(out_pair[v], 2), :, cols], dst_ref=recv.at[v, pl.ds(0, 2), :, cols],
            send_sem=rs_send.at[0, v], recv_sem=rs_recv.at[0, v, k],
            device_id=(first[v], me_s), device_id_type=MESH)

    def step_two(v, cols, k):
        return pltpu.make_async_remote_copy(
            src_ref=fwd.at[v, :, cols], dst_ref=recv.at[v, 2, :, cols],
            send_sem=rs_send.at[1, v], recv_sem=rs_recv.at[1, v, k],
            device_id=(second[v], me_s), device_id_type=MESH)

    for k, cols in enumerate(parts):
        loads[k].wait()
        out = jnp.dot(left, jnp.concatenate(split(xs[:, cols]), axis=0), preferred_element_type=F32)
        out = out[: 4 * nbins] + out[4 * nbins:]
        terms[:, :, :, cols] = out.reshape(2, groups, 2 * nb, step)
        for v in range(2):
            step_one(v, cols, k).start()
        if k == 0:
            for load in load_basis:
                load.start()

    def pass_on(k):
        cols = parts[k]
        for v in range(2):
            step_one(v, cols, k).wait_recv()
            fwd[v, :, cols] = terms[v, pass_slot[v], :, cols] + recv[v, pass_at[v], :, cols]
            step_two(v, cols, k).start()

    two = 2 * rows
    ri, ci = iota((two, two), 0), iota((two, two), 1)
    same_v = mod(ri, 2) + 2 * div(ri, rows) == mod(ci, 2) + 2 * div(ci, rows)
    r_c, c_c = mod(div(ri, 2 * rank), 2), mod(div(ci, 2 * rank), 2)
    keep_re = jnp.where(jnp.logical_and(same_v, r_c == c_c), 1.0, 0.0)
    keep_im = jnp.where(jnp.logical_and(same_v, r_c != c_c), jnp.where(r_c == 0, 1.0, -1.0), 0.0)
    pr, pc = iota((2 * two, 128), 0), iota((2 * two, 128), 1)
    place = ones_where(pc == mod(div(pr, 2), rank) + 2 * rank * mod(div(pr, rows), 2) + rank * div(pr, two))
    fold = ones_where(iota((rank, 3 * two), 0) == mod(div(iota((rank, 3 * two), 1), 2), rank))
    bigs = []
    for p in range(nb // 2):
        load_basis[p].wait()
        w = ub[pl.ds(p * two, two), :]
        bigs.append(dot_nt(w, w))
        for k in range(p * CHUNKS // (nb // 2), (p + 1) * CHUNKS // (nb // 2)):
            pass_on(k)
    lane = iota((rank, 128), 1)
    upper = mod(lane, rank) >= iota((rank, 128), 0)
    packs = []
    for big in bigs:
        wide = right_pick(jnp.concatenate([big * keep_re, big * keep_im], axis=1), place)
        both = jnp.dot(fold, jnp.concatenate(split3(wide), axis=0), preferred_element_type=F32)
        packs.append(jnp.where(upper, both, pltpu.roll(both, 128 - rank, 1)))
    gbuf[me_s] = jnp.where(mod(lane, 2 * rank) < rank, packs[0], pltpu.roll(packs[1], rank, 1))

    def to_all(src, dst, send_sem, recv_sem):
        for d in range(1, spread):
            peer = lax.rem(me_s + d, spread)
            pltpu.make_async_remote_copy(
                src_ref=src(peer), dst_ref=dst, send_sem=send_sem, recv_sem=recv_sem,
                device_id=(me_t, peer), device_id_type=MESH).start()

    def wait_all(like, sem):
        pltpu.make_async_copy(like, like, sem).wait()

    others = pl.ds(0, spread - 1)
    to_all(lambda peer: gbuf.at[me_s], gbuf.at[me_s], sa_sem.at[0], sa_sem.at[1])

    er, ec = iota((nb * rows, 128), 0), iota((nb * rows, 128), 1)
    pick = ones_where(mod(div(er, 2), rank) == ec)
    acc = jnp.zeros((8 * nb, nb * rows), F32)
    square = jnp.zeros((2 * nb, 128), F32)
    for k, cols in enumerate(parts):
        for v in range(2):
            step_two(v, cols, k).wait_recv()
        spec = jnp.stack([terms[v, own_slot[v], :, cols] + recv[v, own_at[v], :, cols] + recv[v, 2, :, cols]
                          for v in range(2)])
        sq = spec[0] * spec[0] + spec[1] * spec[1]
        for i in range(step // 128):
            square = square + sq[:, i * 128:(i + 1) * 128]
        both = jnp.concatenate(split(spec.reshape(4 * nb, step)), axis=0)
        spec_ref[:, cols] = both
        acc = acc + dot_nt(both, ub[:, cols])
    acc = acc[: 4 * nb] + acc[4 * nb:]
    ar, ac = iota((2 * nb, nb * rows), 0), iota((2 * nb, nb * rows), 1)
    acc = jnp.where(mod(ac, 2) == 0, acc[: 2 * nb], acc[2 * nb:])
    even = mod(ar, 2) == 0
    other = jnp.where(even, pltpu.roll(acc, 2 * nb - 1, 0), -pltpu.roll(acc, 1, 0))
    acc = jnp.where(mod(div(ac, 2 * rank), 2) == 0, acc, other)
    coef = right_pick(jnp.where(div(ar, 2) == div(ac, rows), acc, 0.0), pick)
    norm = jnp.sum(square, axis=1, keepdims=True)
    cbuf[me_s] = jnp.where(iota((2 * nb, 128), 1) == rank, norm, coef)
    to_all(lambda peer: cbuf.at[me_s], cbuf.at[me_s], sa_sem.at[2], sa_sem.at[3])
    every = pl.ds(0, points)
    for v in range(2):
        step_one(v, every, 0).wait_send()
        step_two(v, every, 0).wait_send()
    wait_all(gbuf.at[others], sa_sem.at[0])
    wait_all(gbuf.at[others], sa_sem.at[1])
    gram = gbuf[0]
    for s in range(1, spread):
        gram = gram + gbuf[s]
    gram_ref[...] = gram
    wait_all(cbuf.at[others], sa_sem.at[2])
    wait_all(cbuf.at[others], sa_sem.at[3])
    coef = cbuf[0]
    for s in range(1, spread):
        coef = coef + cbuf[s]
    coef_ref[...] = coef


def update(count_ref, eig_ref, coef_ref, gram_ref, spec_ref, ub, fresh_ref, coh_ref, ob, out_sem):
    nb, _, rank = fresh_ref.shape[:3]
    points = fresh_ref.shape[4]
    rows = 4 * rank
    flat_out = fresh_ref.reshape(nb * rows, points)
    halves = [pl.ds(h * 2 * rank, 2 * rank) for h in range(2 * nb)]
    stores = [pltpu.make_async_copy(ob.at[h], flat_out.at[h], out_sem.at[i]) for i, h in enumerate(halves)]
    coef = coef_ref[...]
    count = count_ref[...].astype(F32)
    w_old = count / (count + 1.0)
    w_new = 1.0 / (count + 1.0)
    scaled = w_old * eig_ref[...]
    coef_t = jnp.transpose(coef)
    scaled_t = jnp.transpose(jnp.concatenate([scaled, scaled], axis=0))
    eye = iota((rank, rank), 0) == iota((rank, rank), 1)
    upper = iota((rank, rank), 0) <= iota((rank, rank), 1)
    lower = iota((rank, rank), 0) > iota((rank, rank), 1)
    gram = gram_ref[...]
    gram_t = jnp.transpose(gram)
    r8 = iota((2 * nb, 128), 0)
    k_p = jnp.zeros((2 * nb, 128), F32)
    k_s = jnp.zeros((2 * nb, 128), F32)
    k_a = jnp.zeros((2 * nb, 128), F32)
    pad = jnp.zeros((1, 128 - rank), F32)
    for b in range(nb):
        at = 2 * rank * (b % 2) + rank * (b // 2)
        g, g_t = gram[:, at:at + rank], gram_t[at:at + rank]
        g_re = jnp.where(upper, g, g_t)
        g_im = jnp.where(lower, g, jnp.where(eye, 0.0, -g_t))
        cr, ci = coef[2 * b:2 * b + 1, :rank], coef[2 * b + 1:2 * b + 2, :rank]
        cr_c, ci_c = coef_t[:rank, 2 * b:2 * b + 1], coef_t[:rank, 2 * b + 1:2 * b + 2]
        norm = coef[2 * b:2 * b + 1, rank:rank + 1] + coef[2 * b + 1:2 * b + 2, rank:rank + 1]
        a, a_c = scaled[b:b + 1], scaled_t[:, b:b + 1]
        weight = w_new * (a_c + a) + (w_new * w_new) * norm
        pair = a_c * a
        full_re = pair * g_re + weight * (cr_c * cr + ci_c * ci)
        full_im = pair * g_im + weight * (ci_c * cr - cr_c * ci)
        diag = jnp.where(eye, full_re, 0.0)
        inv = 1.0 / jnp.sqrt(jnp.sum(diag, axis=0, keepdims=True) + 1e-06)
        inv_c = 1.0 / jnp.sqrt(jnp.sum(diag, axis=1, keepdims=True) + 1e-06)
        outer = inv_c * inv
        coh_ref[b, 0] = full_re * outer
        coh_ref[b, 1] = full_im * outer
        p_row = jnp.concatenate([inv * w_new * cr, pad], axis=1)
        q_row = jnp.concatenate([inv * w_new * ci, pad], axis=1)
        a_row = jnp.concatenate([inv * a, pad], axis=1)
        k_p = jnp.where(r8 == 2 * b, p_row, jnp.where(r8 == 2 * b + 1, q_row, k_p))
        k_s = jnp.where(r8 == 2 * b, -q_row, jnp.where(r8 == 2 * b + 1, p_row, k_s))
        k_a = jnp.where(r8 == 2 * b, a_row, k_a)
    wide = 12 * nb
    lane = iota((2 * nb, 128), 1)
    k_mix = jnp.where(lane < rank, k_p, pltpu.roll(k_s, rank, 1))
    k_gain = jnp.where(lane < rank, k_a, pltpu.roll(k_a, rank, 1))
    er, ec = iota((nb * rows, 128), 0), iota((nb * rows, 128), 1)
    pick = ones_where(mod(div(er, 2), 2 * rank) == ec)
    values = jnp.concatenate([k_mix] * 6 + [k_gain], axis=0)
    spread_out = dot_nt(jnp.concatenate([pick] * 3, axis=1), jnp.concatenate(split3(values), axis=1))
    rr, rc = iota(spread_out.shape, 0), iota(spread_out.shape, 1)
    match = div(rr, rows) == mod(div(rc, 2), nb)
    gain = jnp.sum(jnp.where(jnp.logical_and(match, jnp.logical_and(rc >= wide, mod(rc, 2) == 0)), spread_out, 0.0),
                   axis=1, keepdims=True)
    match = jnp.logical_and(match, mod(rr, 2) == mod(div(rc, 2 * nb), 2))
    mix = jnp.where(match, spread_out, 0.0)[:, :wide]
    mh = mix.astype(BF).astype(F32)
    left = jnp.where(rc[:, :wide] < 8 * nb, mh, mix - mh).astype(BF)
    step = 512
    for i, h in enumerate(halves):
        at = i * 2 * rank
        lh, gh = left[at:at + 2 * rank], gain[at:at + 2 * rank]
        for k in range(points // step):
            cols = pl.ds(k * step, step)
            right = jnp.concatenate([spec_ref[:, cols], spec_ref[: 4 * nb, cols]], axis=0)
            add = jnp.dot(lh, right, preferred_element_type=F32)
            ob[h, cols] = (gh * ub[h, cols].astype(F32) + add).astype(BF)
        stores[i].start()
    for store in stores:
        store.wait()


def local(groups, spread, snapshots, bins, eigenvalues, old_basis, block_count):
    slice_len, _, points = snapshots.shape
    nb, _, rank = old_basis.shape[:3]
    rows = 4 * rank
    assert nb * rank == 128
    vmem = pl.BlockSpec(memory_space=pltpu.VMEM)
    hbm = pl.BlockSpec(memory_space=pl.ANY)
    spec, coef, gram, flat = pl.pallas_call(
        functools.partial(exchange, groups, spread),
        out_shape=(
            jax.ShapeDtypeStruct((8 * nb, points), BF),
            jax.ShapeDtypeStruct((2 * nb, 128), F32),
            jax.ShapeDtypeStruct((rank, 128), F32),
            jax.ShapeDtypeStruct((nb * rows, points), BF),
        ),
        in_specs=[pl.BlockSpec(memory_space=pltpu.HBM)] * 3,
        out_specs=(vmem, vmem, vmem, vmem),
        scratch_shapes=[
            pltpu.SMEM(bins.shape, jnp.int32),
            pltpu.VMEM((2 * slice_len, points), F32),
            pltpu.VMEM((2, groups, 2 * nb, points), F32),
            pltpu.VMEM((2, 3, 2 * nb, points), F32),
            pltpu.VMEM((2, 2 * nb, points), F32),
            pltpu.VMEM((spread, 2 * nb, 128), F32),
            pltpu.VMEM((spread, rank, 128), F32),
            pltpu.SemaphoreType.DMA((CHUNKS,)),
            pltpu.SemaphoreType.DMA((nb // 2 + 1,)),
            pltpu.SemaphoreType.DMA((2, 2)),
            pltpu.SemaphoreType.DMA((2, 2, CHUNKS)),
            pltpu.SemaphoreType.DMA((4,)),
        ],
        compiler_params=pltpu.CompilerParams(
            collective_id=0, has_side_effects=True, vmem_limit_bytes=LIMIT),
        name="exchange",
    )(*(pltpu.with_memory_space_constraint(x, pltpu.HBM) for x in (bins, snapshots, old_basis)))
    fresh, coherence = pl.pallas_call(
        update,
        out_shape=(
            jax.ShapeDtypeStruct(old_basis.shape, BF),
            jax.ShapeDtypeStruct((nb, 2, rank, rank), F32),
        ),
        in_specs=[vmem, vmem, vmem, vmem, vmem, vmem],
        out_specs=(hbm, vmem),
        scratch_shapes=[
            pltpu.VMEM((nb * rows, points), BF),
            pltpu.SemaphoreType.DMA((2 * nb,)),
        ],
        compiler_params=pltpu.CompilerParams(vmem_limit_bytes=40 * 2**20),
        name="update",
    )(block_count.reshape(1, 1), eigenvalues, coef, gram, spec, flat)
    return fresh, coherence


def solution(mesh):
    groups, spread = mesh.shape["ta"], mesh.shape["sa"]
    return jax.shard_map(
        functools.partial(local, groups, spread),
        mesh=mesh,
        in_specs=(P("ta", None, "sa"), P(), P("ta", None), P("ta", None, None, None, "sa"), P()),
        out_specs=(P("ta", None, None, None, "sa"), P("ta", None, None, None)),
        check_vma=False,
    )
```

```python
import functools
import math

import jax
import jax.numpy as jnp
from jax import lax
from jax.experimental import pallas as pl
from jax.experimental.pallas import tpu as pltpu
from jax.sharding import PartitionSpec as P

MESH = pl.DeviceIdType.MESH
BF = jnp.bfloat16
F32 = jnp.float32
CHUNKS = 8
LIMIT = 40 * 2**20


def dot_nt(a, b):
    return lax.dot_general(a, b, (((1,), (1,)), ((), ())), preferred_element_type=F32)


def split(x):
    high = x.astype(BF)
    return high, (x - high.astype(F32)).astype(BF)


def split3(x):
    high = x.astype(BF)
    rest = x - high.astype(F32)
    mid = rest.astype(BF)
    return high, mid, (rest - mid.astype(F32)).astype(BF)


def right_pick(x, pick):
    n = x.shape[0]
    out = jnp.dot(jnp.concatenate(split3(x), axis=0), pick, preferred_element_type=F32)
    return out[:n] + out[n:2 * n] + out[2 * n:]


def iota(shape, axis):
    return lax.broadcasted_iota(jnp.int32, shape, axis)


def div(x, n):
    assert n & (n - 1) == 0
    return lax.shift_right_logical(x, jnp.full(x.shape, n.bit_length() - 1, x.dtype))


def mod(x, n):
    assert n & (n - 1) == 0
    return jnp.bitwise_and(x, n - 1)


def ones_where(mask):
    return jnp.where(mask, 1.0, 0.0).astype(BF)


def exchange(groups, spread, bins_ref, snap_ref, basis_ref, spec_ref, coef_ref, gram_ref, ub,
             bins, xs, terms, recv, cbuf, gbuf, in_sem, b_sem, rs_send, rs_recv, g_send, g_recv, c_send, c_recv):
    assert groups == 4
    slice_len = snap_ref.shape[0]
    points = snap_ref.shape[2]
    nb, _, rank = basis_ref.shape[:3]
    nbins = bins_ref.shape[0]
    rows = 4 * rank
    step = points // CHUNKS
    total = slice_len * groups
    me_t = lax.axis_index("ta")
    me_s = lax.axis_index("sa")
    load_bins = pltpu.make_async_copy(bins_ref, bins, b_sem.at[2 * nb])
    load_bins.start()
    parts = [pl.ds(k * step, step) for k in range(CHUNKS)]
    loads = [[pltpu.make_async_copy(snap_ref.at[:, v, p], xs.at[v, :, p], in_sem.at[v, k]) for v in range(2)]
             for k, p in enumerate(parts)]
    for pair in loads:
        for load in pair:
            load.start()
    flat = basis_ref.reshape(nb * rows, points)
    halves = [pl.ds(h * 2 * rank, 2 * rank) for h in range(2 * nb)]
    load_basis = [pltpu.make_async_copy(flat.at[h], ub.at[h], b_sem.at[i]) for i, h in enumerate(halves)]

    near = me_t + 1 - 2 * lax.rem(me_t, 2)
    far = lax.rem(me_t + 2, 4)
    diagonal = lax.rem(near + 2, 4)
    barrier = pltpu.get_barrier_semaphore()
    for peer in (near, far, diagonal):
        pl.semaphore_signal(barrier, inc=1, device_id=(peer, me_s), device_id_type=MESH)
    for d in range(1, spread):
        pl.semaphore_signal(barrier, inc=1, device_id=(me_t, lax.rem(me_s + d, spread)), device_id_type=MESH)

    t = iota((2 * nbins, slice_len), 1) + me_t * slice_len
    row = iota((2 * nbins, slice_len), 0)
    unit = 2.0 * math.pi / total
    window = (0.5 - 0.5 * jnp.cos(unit * t[:8].astype(F32))) * math.sqrt(8.0 / (3.0 * total))
    window = jnp.concatenate([window] * (2 * nbins // 8), axis=0)
    load_bins.wait()
    bin_of = jnp.zeros((2 * nbins, slice_len), jnp.int32)
    for b in range(nbins):
        bin_of = jnp.where(div(row, 2) == b, bins[b], bin_of)
    phase = jnp.bitwise_and(bin_of * t + mod(row, 2) * (total // 4), total - 1)
    th, tl = split(jnp.cos(unit * phase.astype(F32)) * window)
    left = jnp.concatenate(
        [jnp.concatenate([th, th], axis=1), jnp.concatenate([tl, jnp.zeros_like(tl)], axis=1)], axis=0)

    pl.semaphore_wait(barrier, 3 + spread - 1)

    def rs_copy(slot, k, peer):
        cols = pl.ds(k * step, step)
        return pltpu.make_async_remote_copy(
            src_ref=terms.at[peer, :, :, cols], dst_ref=recv.at[slot, :, :, cols],
            send_sem=rs_send.at[k, slot], recv_sem=rs_recv.at[k, slot],
            device_id=(peer, me_s), device_id_type=MESH)

    copies = {}
    for k in range(CHUNKS):
        cols = parts[k]
        for v in range(2):
            loads[k][v].wait()
            xh, xl = split(xs[v, :, cols])
            out = jnp.dot(left, jnp.concatenate([xh, xl], axis=0), preferred_element_type=F32)
            out = out[: 2 * nbins] + out[2 * nbins:]
            terms[:, v, :, cols] = out.reshape(groups, 2 * nb, step)
        for slot, peer in enumerate((diagonal, near, far)):
            copies[k, slot] = rs_copy(slot, k, peer)
            copies[k, slot].start()
        if k == 1:
            for load in load_basis:
                load.start()

    two = 2 * rows
    ri, ci = iota((two, two), 0), iota((two, two), 1)
    same_v = mod(ri, 2) + 2 * div(ri, rows) == mod(ci, 2) + 2 * div(ci, rows)
    r_c, c_c = mod(div(ri, 2 * rank), 2), mod(div(ci, 2 * rank), 2)
    keep_re = jnp.where(jnp.logical_and(same_v, r_c == c_c), 1.0, 0.0)
    keep_im = jnp.where(jnp.logical_and(same_v, r_c != c_c), jnp.where(r_c == 0, 1.0, -1.0), 0.0)
    pr, pc = iota((2 * two, 128), 0), iota((2 * two, 128), 1)
    place = ones_where(pc == mod(div(pr, 2), rank) + 2 * rank * mod(div(pr, rows), 2) + rank * div(pr, two))
    fold = ones_where(iota((rank, 3 * two), 0) == mod(div(iota((rank, 3 * two), 1), 2), rank))
    for p in range(nb // 2):
        for load in load_basis[4 * p:4 * p + 4]:
            load.wait()
        w = ub[pl.ds(p * two, two), :]
        big = dot_nt(w, w)
        wide = right_pick(jnp.concatenate([big * keep_re, big * keep_im], axis=1), place)
        gbuf[me_s, p] = jnp.dot(fold, jnp.concatenate(split3(wide), axis=0), preferred_element_type=F32)
    g_copies = []
    for d in range(1, spread):
        copy = pltpu.make_async_remote_copy(
            src_ref=gbuf.at[me_s], dst_ref=gbuf.at[me_s], send_sem=g_send.at[d], recv_sem=g_recv.at[d],
            device_id=(me_t, lax.rem(me_s + d, spread)), device_id_type=MESH)
        copy.start()
        g_copies.append(copy)

    er, ec = iota((nb * rows, 128), 0), iota((nb * rows, 128), 1)
    pick = ones_where(mod(div(er, 2), rank) == ec)
    acc = jnp.zeros((8 * nb, nb * rows), F32)
    square = jnp.zeros((2 * nb, 128), F32)
    for k in range(CHUNKS):
        cols = pl.ds(k * step, step)
        for slot in range(3):
            copies[k, slot].wait_recv()
        spec = (terms[me_t, :, :, cols] + recv[0, :, :, cols]) + (recv[1, :, :, cols] + recv[2, :, :, cols])
        sq = spec[0] * spec[0] + spec[1] * spec[1]
        for i in range(step // 128):
            square = square + sq[:, i * 128:(i + 1) * 128]
        both = jnp.concatenate(split(spec.reshape(4 * nb, step)), axis=0)
        spec_ref[:, cols] = both
        acc = acc + dot_nt(both, ub[:, cols])
    acc = acc[: 4 * nb] + acc[4 * nb:]
    ar, ac = iota((2 * nb, nb * rows), 0), iota((2 * nb, nb * rows), 1)
    acc = jnp.where(mod(ac, 2) == 0, acc[: 2 * nb], acc[2 * nb:])
    even = mod(ar, 2) == 0
    other = jnp.where(even, pltpu.roll(acc, 2 * nb - 1, 0), -pltpu.roll(acc, 1, 0))
    acc = jnp.where(mod(div(ac, 2 * rank), 2) == 0, acc, other)
    coef = right_pick(jnp.where(div(ar, 2) == div(ac, rows), acc, 0.0), pick)
    norm = jnp.sum(square, axis=1, keepdims=True)
    cbuf[me_s] = jnp.where(iota((2 * nb, 128), 1) == rank, norm, coef)
    c_copies = []
    for d in range(1, spread):
        copy = pltpu.make_async_remote_copy(
            src_ref=cbuf.at[me_s], dst_ref=cbuf.at[me_s], send_sem=c_send.at[d], recv_sem=c_recv.at[d],
            device_id=(me_t, lax.rem(me_s + d, spread)), device_id_type=MESH)
        copy.start()
        c_copies.append(copy)
    for copy in g_copies:
        copy.wait_recv()
    gram = gbuf[0]
    for s in range(1, spread):
        gram = gram + gbuf[s]
    gram_ref[...] = gram
    for copy in list(copies.values()) + g_copies:
        copy.wait_send()
    for copy in c_copies:
        copy.wait_recv()
    coef = cbuf[0]
    for s in range(1, spread):
        coef = coef + cbuf[s]
    coef_ref[...] = coef
    for copy in c_copies:
        copy.wait_send()


def update(count_ref, eig_ref, coef_ref, gram_ref, spec_ref, ub, fresh_ref, coh_ref, ob, out_sem):
    nb, _, rank = fresh_ref.shape[:3]
    points = fresh_ref.shape[4]
    rows = 4 * rank
    flat_out = fresh_ref.reshape(nb * rows, points)
    halves = [pl.ds(h * 2 * rank, 2 * rank) for h in range(2 * nb)]
    stores = [pltpu.make_async_copy(ob.at[h], flat_out.at[h], out_sem.at[i]) for i, h in enumerate(halves)]
    count = jnp.full((1, 1), count_ref[0], jnp.int32).astype(F32)
    w_old = count / (count + 1.0)
    w_new = 1.0 / (count + 1.0)
    scaled = w_old * eig_ref[...]
    coef = coef_ref[...]
    coef_t = jnp.transpose(coef)
    scaled_t = jnp.transpose(jnp.concatenate([scaled, scaled], axis=0))
    eye = iota((rank, rank), 0) == iota((rank, rank), 1)
    r8 = iota((2 * nb, 128), 0)
    k_p = jnp.zeros((2 * nb, 128), F32)
    k_s = jnp.zeros((2 * nb, 128), F32)
    k_a = jnp.zeros((2 * nb, 128), F32)
    pad = jnp.zeros((1, 128 - rank), F32)
    for b in range(nb):
        g = gram_ref[b // 2]
        at = 2 * rank * (b % 2)
        g_re, g_im = g[:, at:at + rank], g[:, at + rank:at + 2 * rank]
        cr, ci = coef[2 * b:2 * b + 1, :rank], coef[2 * b + 1:2 * b + 2, :rank]
        cr_c, ci_c = coef_t[:rank, 2 * b:2 * b + 1], coef_t[:rank, 2 * b + 1:2 * b + 2]
        norm = coef[2 * b:2 * b + 1, rank:rank + 1] + coef[2 * b + 1:2 * b + 2, rank:rank + 1]
        a, a_c = scaled[b:b + 1], scaled_t[:, b:b + 1]
        weight = w_new * (a_c + a) + (w_new * w_new) * norm
        pair = a_c * a
        full_re = pair * g_re + weight * (cr_c * cr + ci_c * ci)
        full_im = pair * g_im + weight * (ci_c * cr - cr_c * ci)
        diag = jnp.where(eye, full_re, 0.0)
        inv = 1.0 / jnp.sqrt(jnp.sum(diag, axis=0, keepdims=True) + 1e-06)
        inv_c = 1.0 / jnp.sqrt(jnp.sum(diag, axis=1, keepdims=True) + 1e-06)
        outer = inv_c * inv
        coh_ref[b, 0] = full_re * outer
        coh_ref[b, 1] = full_im * outer
        p_row = jnp.concatenate([inv * w_new * cr, pad], axis=1)
        q_row = jnp.concatenate([inv * w_new * ci, pad], axis=1)
        a_row = jnp.concatenate([inv * a, pad], axis=1)
        k_p = jnp.where(r8 == 2 * b, p_row, jnp.where(r8 == 2 * b + 1, q_row, k_p))
        k_s = jnp.where(r8 == 2 * b, -q_row, jnp.where(r8 == 2 * b + 1, p_row, k_s))
        k_a = jnp.where(r8 == 2 * b, a_row, k_a)
    wide = 12 * nb
    lane = iota((2 * nb, 128), 1)
    k_mix = jnp.where(lane < rank, k_p, pltpu.roll(k_s, rank, 1))
    k_gain = jnp.where(lane < rank, k_a, pltpu.roll(k_a, rank, 1))
    er, ec = iota((nb * rows, 128), 0), iota((nb * rows, 128), 1)
    pick = ones_where(mod(div(er, 2), 2 * rank) == ec)
    values = jnp.concatenate([k_mix] * 6 + [k_gain], axis=0)
    spread_out = dot_nt(jnp.concatenate([pick] * 3, axis=1), jnp.concatenate(split3(values), axis=1))
    rr, rc = iota(spread_out.shape, 0), iota(spread_out.shape, 1)
    match = div(rr, rows) == mod(div(rc, 2), nb)
    gain = jnp.sum(jnp.where(jnp.logical_and(match, jnp.logical_and(rc >= wide, mod(rc, 2) == 0)), spread_out, 0.0),
                   axis=1, keepdims=True)
    match = jnp.logical_and(match, mod(rr, 2) == mod(div(rc, 2 * nb), 2))
    mix = jnp.where(match, spread_out, 0.0)[:, :wide]
    mh = mix.astype(BF).astype(F32)
    left = jnp.where(rc[:, :wide] < 8 * nb, mh, mix - mh).astype(BF)
    step = 512
    for i, h in enumerate(halves):
        at = i * 2 * rank
        lh, gh = left[at:at + 2 * rank], gain[at:at + 2 * rank]
        for k in range(points // step):
            cols = pl.ds(k * step, step)
            right = jnp.concatenate([spec_ref[:, cols], spec_ref[: 4 * nb, cols]], axis=0)
            add = jnp.dot(lh, right, preferred_element_type=F32)
            ob[h, cols] = (gh * ub[h, cols].astype(F32) + add).astype(BF)
        stores[i].start()
    for store in stores:
        store.wait()


def local(groups, spread, snapshots, bins, eigenvalues, old_basis, block_count):
    slice_len, _, points = snapshots.shape
    nb, _, rank = old_basis.shape[:3]
    rows = 4 * rank
    vmem = pl.BlockSpec(memory_space=pltpu.VMEM)
    smem = pl.BlockSpec(memory_space=pltpu.SMEM)
    hbm = pl.BlockSpec(memory_space=pl.ANY)
    spec, coef, gram, flat = pl.pallas_call(
        functools.partial(exchange, groups, spread),
        out_shape=(
            jax.ShapeDtypeStruct((8 * nb, points), BF),
            jax.ShapeDtypeStruct((2 * nb, 128), F32),
            jax.ShapeDtypeStruct((nb // 2, rank, 128), F32),
            jax.ShapeDtypeStruct((nb * rows, points), BF),
        ),
        in_specs=[pl.BlockSpec(memory_space=pltpu.HBM)] * 3,
        out_specs=(vmem, vmem, vmem, vmem),
        scratch_shapes=[
            pltpu.SMEM(bins.shape, jnp.int32),
            pltpu.VMEM((2, slice_len, points), F32),
            pltpu.VMEM((groups, 2, 2 * nb, points), F32),
            pltpu.VMEM((3, 2, 2 * nb, points), F32),
            pltpu.VMEM((spread, 2 * nb, 128), F32),
            pltpu.VMEM((spread, nb // 2, rank, 128), F32),
            pltpu.SemaphoreType.DMA((2, CHUNKS)),
            pltpu.SemaphoreType.DMA((2 * nb + 1,)),
            pltpu.SemaphoreType.DMA((CHUNKS, 3)),
            pltpu.SemaphoreType.DMA((CHUNKS, 3)),
            pltpu.SemaphoreType.DMA((spread,)),
            pltpu.SemaphoreType.DMA((spread,)),
            pltpu.SemaphoreType.DMA((spread,)),
            pltpu.SemaphoreType.DMA((spread,)),
        ],
        compiler_params=pltpu.CompilerParams(
            collective_id=0, has_side_effects=True, vmem_limit_bytes=LIMIT),
        name="exchange",
    )(*(pltpu.with_memory_space_constraint(x, pltpu.HBM) for x in (bins, snapshots, old_basis)))
    fresh, coherence = pl.pallas_call(
        update,
        out_shape=(
            jax.ShapeDtypeStruct(old_basis.shape, BF),
            jax.ShapeDtypeStruct((nb, 2, rank, rank), F32),
        ),
        in_specs=[smem, vmem, vmem, vmem, vmem, vmem],
        out_specs=(hbm, vmem),
        scratch_shapes=[
            pltpu.VMEM((nb * rows, points), BF),
            pltpu.SemaphoreType.DMA((2 * nb,)),
        ],
        compiler_params=pltpu.CompilerParams(vmem_limit_bytes=40 * 2**20),
        name="update",
    )(block_count, eigenvalues, coef, gram, spec, flat)
    return fresh, coherence


def solution(mesh):
    groups, spread = mesh.shape["ta"], mesh.shape["sa"]
    return jax.shard_map(
        functools.partial(local, groups, spread),
        mesh=mesh,
        in_specs=(P("ta", None, "sa"), P(), P("ta", None), P("ta", None, None, None, "sa"), P()),
        out_specs=(P("ta", None, None, None, "sa"), P("ta", None, None, None)),
        check_vma=False,
    )
```
